32 devices in a mesh: dp: 16 (over z, y, core), fsdp: 2 (over x).
Axes of the slice: x: 2, y: 2, z: 4, core: 2. Of those that a mesh axis runs over, the one named last changes fastest.
Arguments:
- block_input: bfloat16 [512, 784, 192], P(('dp', 'fsdp')), may hold values from -6 to 6
- token_crop: int32 [512, 784], P(('dp', 'fsdp')), may hold values from 0 to 3, as said below
- key_crop: int32 [512, 196], P(('dp', 'fsdp')), may hold values from 0 to 3, as said below
- first_gain: float32 [192], replicated, may hold values from 0.25 to 1.75
- first_bias: float32 [192], replicated, may hold values from -1.75 to 1.75
- qkv_weight: bfloat16 [192, 576], P('fsdp', 'dp'), may hold values from -0.4375 to 0.4375
- qkv_bias: float32 [576], replicated, may hold values from -1.75 to 1.75
- pool_kernel: float32 [2, 9, 96], replicated, may hold values from -2 to 2
- pool_gain: float32 [2, 96], replicated, may hold values from 0.25 to 1.75
- pool_bias: float32 [2, 96], replicated, may hold values from -1.75 to 1.75
- rel_height: float32 [55, 96], replicated, may hold values from -0.625 to 0.625
- rel_width: float32 [55, 96], replicated, may hold values from -0.625 to 0.625
- proj_weight: bfloat16 [192, 192], P('fsdp', 'dp'), may hold values from -0.4375 to 0.4375
- proj_bias: float32 [192], replicated, may hold values from -1.75 to 1.75
- second_gain: float32 [192], replicated, may hold values from 0.25 to 1.75
- second_bias: float32 [192], replicated, may hold values from -1.75 to 1.75
- fc1_weight: bfloat16 [192, 768], P('fsdp', 'dp'), may hold values from -0.4375 to 0.4375
- fc1_bias: float32 [768], replicated, may hold values from -3 to 3
- fc2_weight: bfloat16 [768, 192], P('fsdp', 'dp'), may hold values from -0.21875 to 0.21875
- fc2_bias: float32 [192], replicated, may hold values from -1.75 to 1.75
- cotangent: bfloat16 [512, 784, 192], P(('dp', 'fsdp')), may hold values from -18 to 18
Outputs:
- block_output: bfloat16 [512, 784, 192], P(('dp', 'fsdp'))
- input_grad: float32 [512, 784, 192], P(('dp', 'fsdp'))
- grad_first_gain: float32 [192], replicated
- grad_first_bias: float32 [192], replicated
- grad_qkv_weight: float32 [192, 576], P('fsdp', 'dp')
- grad_qkv_bias: float32 [576], replicated
- grad_pool_kernel: float32 [2, 9, 96], replicated
- grad_pool_gain: float32 [2, 96], replicated
- grad_pool_bias: float32 [2, 96], replicated
- grad_rel_height: float32 [55, 96], replicated
- grad_rel_width: float32 [55, 96], replicated
- grad_proj_weight: float32 [192, 192], P('fsdp', 'dp')
- grad_proj_bias: float32 [192], replicated
- grad_second_gain: float32 [192], replicated
- grad_second_bias: float32 [192], replicated
- grad_fc1_weight: float32 [192, 768], P('fsdp', 'dp')
- grad_fc1_bias: float32 [768], replicated
- grad_fc2_weight: float32 [768, 192], P('fsdp', 'dp')
- grad_fc2_bias: float32 [192], replicated
The draws below stay inside these ranges and needn't reach their ends.
Inputs may be any that keep to these rules, and one draw needn't show every extreme that they name: `token_crop`: each canvas is cut into four rectangular crops by one row cut and one column cut, each at an even position from 2 to 26; a token's crop id is 2 (row at or below the row cut) + (column at or right of the column cut). `key_crop`: pooled key (i, j) of a canvas carries the crop id of token (2 i, 2 j) of that canvas.
All inputs are finite; a program needn't handle non-finite values.
Results may differ from the reference program's by a relative error of at most 0.017.
Values may be sent and summed in bfloat16 or wider, within the bound.
A program may use at most 384 MiB of HBM per device.

```python
import jax
import jax.numpy as jnp
from jax import lax

D = 192
HEADS = 2
HD = 96
FF = 768
SIDE = 28
KS = 14
NTOK = 784
NKEY = 196
REL = 55
CANVASES = 512


def crop_layout(key):
    cuts = 2 * jax.random.randint(jax.random.fold_in(key, 11), (CANVASES, 2), 1, SIDE // 2)
    positions = jnp.arange(SIDE, dtype=jnp.int32)
    lower = (positions[None, :] >= cuts[:, 0:1]).astype(jnp.int32)
    right_side = (positions[None, :] >= cuts[:, 1:2]).astype(jnp.int32)
    return 2 * lower[:, :, None] + right_side[:, None, :]


def draw_token_crop(key, part):
    return crop_layout(key).reshape(CANVASES, NTOK)


def draw_key_crop(key, part):
    return crop_layout(key)[:, ::2, ::2].reshape(CANVASES, NKEY)


def draw_cotangent(key, part):
    key = jax.random.fold_in(key, 5)
    rising = 1.0 + 2.0 * jnp.arange(CANVASES, dtype=jnp.float32) / max(CANVASES - 1, 1)
    base = jnp.clip(jax.random.normal(key, (CANVASES, NTOK, D), jnp.float32), -6.0, 6.0)
    return (base * rising[:, None, None]).astype(jnp.bfloat16)


def levels(stream_key, extent, shards, low, high):
    level = 1.0
    for position, parts in shards:
        steps = jax.random.uniform(jax.random.fold_in(jax.random.fold_in(stream_key, 6), position), (parts,), jnp.float32, low / len(shards), high / len(shards))
        level = level * jnp.repeat(jnp.exp(steps), extent[position] // parts).reshape((-1,) + (1,) * (len(extent) - 1 - position))
    return level


def scatter_about(key, shape, scale, reach, shards=(), kind=jnp.bfloat16):
    factor_of = levels(key, shape, shards, -0.22, 0.18) if shards else 1.0
    values = jax.random.normal(key, shape, jnp.float32) * scale * factor_of
    return jnp.minimum(jnp.maximum(values, -reach), reach).astype(kind)


def setup_inputs(seed: int = 0) -> dict:
    keys = jax.random.split(jax.random.key(seed), 22)
    block_input = scatter_about(keys[0], (CANVASES, NTOK, D), 1.0, 6.0, ((0, 32),))
    token_crop = draw_token_crop(jax.random.fold_in(keys[21], 71), 0)
    key_crop = draw_key_crop(jax.random.fold_in(keys[21], 71), 0)
    first_gain = jnp.clip(1.0 + 0.15 * jax.random.normal(keys[3], (D,), jnp.float32), 0.25, 1.75)
    first_bias = scatter_about(keys[4], (D,), 0.3, 1.75, (), jnp.float32)
    qkv_weight = scatter_about(keys[5], (D, 3 * D), D ** -0.5, 0.4375, ((0, 2), (1, 16)))
    qkv_bias = scatter_about(keys[6], (3 * D,), 0.3, 1.75, (), jnp.float32)
    pool_kernel = scatter_about(keys[7], (2, 9, HD), 9 ** -0.5, 2.0, (), jnp.float32)
    pool_gain = jnp.clip(1.0 + 0.15 * jax.random.normal(keys[8], (2, HD), jnp.float32), 0.25, 1.75)
    pool_bias = scatter_about(keys[9], (2, HD), 0.3, 1.75, (), jnp.float32)
    rel_height = scatter_about(keys[10], (REL, HD), 0.1, 0.625, (), jnp.float32)
    rel_width = scatter_about(keys[11], (REL, HD), 0.1, 0.625, (), jnp.float32)
    proj_weight = scatter_about(keys[12], (D, D), D ** -0.5, 0.4375, ((0, 2), (1, 16)))
    proj_bias = scatter_about(keys[13], (D,), 0.3, 1.75, (), jnp.float32)
    second_gain = jnp.clip(1.0 + 0.15 * jax.random.normal(keys[14], (D,), jnp.float32), 0.25, 1.75)
    second_bias = scatter_about(keys[15], (D,), 0.3, 1.75, (), jnp.float32)
    fc1_weight = scatter_about(keys[16], (D, FF), D ** -0.5, 0.4375, ((0, 2), (1, 16)))
    fc1_bias = scatter_about(keys[17], (FF,), 0.5, 3.0, (), jnp.float32)
    fc2_weight = scatter_about(keys[18], (FF, D), FF ** -0.5, 0.21875, ((0, 2), (1, 16)))
    fc2_bias = scatter_about(keys[19], (D,), 0.3, 1.75, (), jnp.float32)
    cotangent = draw_cotangent(jax.random.fold_in(keys[21], 71), 0)
    return dict(block_input=block_input, token_crop=token_crop, key_crop=key_crop, first_gain=first_gain, first_bias=first_bias, qkv_weight=qkv_weight, qkv_bias=qkv_bias, pool_kernel=pool_kernel, pool_gain=pool_gain, pool_bias=pool_bias, rel_height=rel_height, rel_width=rel_width, proj_weight=proj_weight, proj_bias=proj_bias, second_gain=second_gain, second_bias=second_bias, fc1_weight=fc1_weight, fc1_bias=fc1_bias, fc2_weight=fc2_weight, fc2_bias=fc2_bias, cotangent=cotangent)


layer_eps = 1e-06
masked_fill = -1e+30
highest = lax.Precision.HIGHEST

@jax.custom_vjp
def low(v):
    return lax.optimization_barrier(v.astype(jnp.bfloat16)).astype(jnp.float32)

@jax.custom_vjp
def low_back(v):
    return v

def low_keep(v):
    return (low(v), None)

def low_pass(kept, grad):
    return (grad,)

def back_keep(v):
    return (v, None)

def back_low(kept, grad):
    return (low(grad),)
low.defvjp(low_keep, low_pass)
low_back.defvjp(back_keep, back_low)

def layer_norm(values, norm_gain, norm_shift):
    center = values - lax.optimization_barrier(jnp.mean(values, -1, keepdims=True))
    spread = lax.optimization_barrier(jnp.mean(center * center, -1, keepdims=True))
    return center * lax.rsqrt(spread + layer_eps) * norm_gain + norm_shift

def pool_norm(field, kernel, norm_gain, norm_shift):
    padded = jnp.pad(field, ((0, 0), (1, 1), (1, 1), (0, 0), (0, 0)))
    pooled = 0.0
    for row_tap in range(3):
        for col_tap in range(3):
            pooled = pooled + padded[:, row_tap:row_tap + SIDE:2, col_tap:col_tap + SIDE:2] * kernel[3 * row_tap + col_tap]
    return layer_norm(pooled, norm_gain, norm_shift)

def gelu_exact(values):
    return jax.nn.gelu(values, approximate=False)

def matmul(left, right):
    return jnp.dot(left, right, preferred_element_type=jnp.float32, precision=highest)

def block_forward(inputs, token_ids, key_ids, params):
    first_gain, first_bias, qkv_weight, qkv_bias, pool_kernel, pool_gain, pool_bias, rel_height, rel_width, proj_weight, proj_bias, second_gain, second_bias, fc1_weight, fc1_bias, fc2_weight, fc2_bias = params
    canvas_count = inputs.shape[0]
    token_rows = inputs.reshape(canvas_count * NTOK, D)
    normed = low(layer_norm(token_rows, first_gain, first_bias))
    packed = low_back(matmul(normed, qkv_weight) + qkv_bias).reshape(canvas_count, NTOK, 3, HEADS, HD)
    queries = low(packed[:, :, 0])
    grid_shape = (canvas_count, SIDE, SIDE, HEADS, HD)
    keys_pooled = low(pool_norm(packed[:, :, 1].reshape(grid_shape), pool_kernel[0], pool_gain[0], pool_bias[0]))
    keys_pooled = keys_pooled.reshape(canvas_count, NKEY, HEADS, HD)
    values_pooled = low(pool_norm(packed[:, :, 2].reshape(grid_shape), pool_kernel[1], pool_gain[1], pool_bias[1]))
    values_pooled = values_pooled.reshape(canvas_count, NKEY, HEADS, HD)
    table_index = jnp.arange(SIDE, dtype=jnp.int32)[:, None] - 2 * jnp.arange(KS, dtype=jnp.int32)[None, :] + 2 * (KS - 1)
    rows_h = rel_height[table_index]
    rows_w = rel_width[table_index]
    content = jnp.einsum('cqhd,ckhd->chqk', queries, keys_pooled, precision=highest) * HD ** (-0.5)
    grid_q = queries.reshape(grid_shape)
    along_h = jnp.einsum('cxyhd,xkd->chxyk', grid_q, rows_h, precision=highest)
    along_w = jnp.einsum('cxyhd,ykd->chxyk', grid_q, rows_w, precision=highest)
    scores = content.reshape(canvas_count, HEADS, SIDE, SIDE, KS, KS) + along_h[..., :, None] + along_w[..., None, :]
    scores = scores.reshape(canvas_count, HEADS, NTOK, NKEY)
    same_crop = token_ids[:, None, :, None] == key_ids[:, None, None, :]
    scores = low_back(jnp.where(same_crop, scores, masked_fill))
    row_max = lax.optimization_barrier(jnp.max(scores, -1, keepdims=True))
    exponent = jnp.exp(scores - row_max)
    probs = low(exponent / lax.optimization_barrier(jnp.sum(exponent, -1, keepdims=True)))
    mixed_heads = jnp.einsum('chqk,ckhd->cqhd', probs, values_pooled, precision=highest) + queries
    attended = low(low_back(mixed_heads)).reshape(canvas_count * NTOK, D)
    middle = token_rows + low_back(matmul(attended, proj_weight) + proj_bias)
    normed_second = low(layer_norm(middle, second_gain, second_bias))
    hidden = low_back(matmul(normed_second, fc1_weight) + fc1_bias)
    activated = low(gelu_exact(hidden))
    output = middle + low_back(matmul(activated, fc2_weight) + fc2_bias)
    return output.reshape(canvas_count, NTOK, D)

def reference(block_input, token_crop, key_crop, first_gain, first_bias, qkv_weight, qkv_bias, pool_kernel, pool_gain, pool_bias, rel_height, rel_width, proj_weight, proj_bias, second_gain, second_bias, fc1_weight, fc1_bias, fc2_weight, fc2_bias, cotangent):
    params = tuple((weight.astype(jnp.float32) for weight in (first_gain, first_bias, qkv_weight, qkv_bias, pool_kernel, pool_gain, pool_bias, rel_height, rel_width, proj_weight, proj_bias, second_gain, second_bias, fc1_weight, fc1_bias, fc2_weight, fc2_bias)))
    group_count = CANVASES // 4
    inputs = block_input.astype(jnp.float32).reshape(group_count, 4, NTOK, D)
    crop_groups = token_crop.reshape(group_count, 4, NTOK)
    key_groups = key_crop.reshape(group_count, 4, NKEY)

    def whole_forward(group_inputs, group_params):

        def group_step(canvas_item):
            return jax.checkpoint(block_forward)(canvas_item[0], canvas_item[1], canvas_item[2], group_params)
        return lax.map(group_step, (group_inputs, crop_groups, key_groups))
    output, pullback = jax.vjp(whole_forward, inputs, params)
    grad_inputs, grad_params = pullback(cotangent.astype(jnp.float32).reshape(group_count, 4, NTOK, D))
    return (output.reshape(CANVASES, NTOK, D).astype(jnp.bfloat16), grad_inputs.reshape(CANVASES, NTOK, D), grad_params[0], grad_params[1], grad_params[2], grad_params[3], grad_params[4], grad_params[5], grad_params[6], grad_params[7], grad_params[8], grad_params[9], grad_params[10], grad_params[11], grad_params[12], grad_params[13], grad_params[14], grad_params[15], grad_params[16])
```

```python
import jax
import jax.numpy as jnp
from jax import lax
from jax.experimental import pallas as pl
from jax.experimental.pallas import tpu as pltpu
from jax.sharding import PartitionSpec as P

D = 192
HEADS = 2
HD = 96
FF = 768
SIDE = 28
KS = 14
NTOK = 784
NKEY = 196
REL = 55

EPS = 1e-06
FILL = -1e30
LOG2E = 1.4426950408889634
LN2 = 0.6931471805599453
SCALE = HD ** (-0.5)
BASE = 32
KVROWS = BASE + NTOK + 24
bf = jnp.bfloat16
PAIR = 2
SKEW = 3
FEAT = 208
f32 = jnp.float32


def dot(a, b):
    return jnp.dot(a, b, preferred_element_type=f32)


def dot_nt(a, b):
    return lax.dot_general(a, b, (((1,), (1,)), ((), ())), preferred_element_type=f32)


def dot_tn(a, b):
    return lax.dot_general(a, b, (((0,), (0,)), ((), ())), preferred_element_type=f32)


def iota(shape, dim):
    return lax.broadcasted_iota(jnp.int32, shape, dim)


def widen(v):
    return jnp.concatenate([v, jnp.zeros((v.shape[0], 256 - v.shape[1]), v.dtype)], axis=1)


def lanes(col):
    return jnp.concatenate([col] * 6 + [col[:, :16]], axis=1)


def fold_lanes(v):
    total = v[:, 0:128]
    for n in range(1, 6):
        total = total + v[:, 128 * n:128 * n + 128]
    return total


def add_lanes(ref, tail, n, v):
    ref[n] += fold_lanes(v)
    tail[n] += v[:, 768:784]


def with_ones(v):
    extra = (iota((16, NTOK), 0) < 2).astype(f32).astype(bf)
    return jnp.concatenate([v, extra], 0)


def norm_cols(v):
    mean = jnp.sum(v, 0, keepdims=True) * (1.0 / D)
    c = v - mean
    var = jnp.sum(c * c, 0, keepdims=True) * (1.0 / D)
    r = lax.rsqrt(var + EPS)
    return c * r, r


def norm_cols_back(ge, u, r):
    s1 = jnp.sum(ge, 0, keepdims=True) * (1.0 / D)
    s2 = jnp.sum(ge * u, 0, keepdims=True) * (1.0 / D)
    return (ge - s1 - u * s2) * r


def fold(v):
    total = v[0:8]
    for n in range(1, v.shape[0] // 8):
        total = total + v[8 * n:8 * n + 8]
    return total


def norm_parts(v, mask, width):
    mean = jnp.sum(v, -1, keepdims=True) * (1.0 / width)
    c = (v - mean) * mask
    var = jnp.sum(c * c, -1, keepdims=True) * (1.0 / width)
    r = lax.rsqrt(var + EPS)
    return c * r, r


def norm_back(ge, u, r, width):
    s1 = jnp.sum(ge, -1, keepdims=True) * (1.0 / width)
    s2 = jnp.sum(ge * u, -1, keepdims=True) * (1.0 / width)
    return (ge - s1 - u * s2) * r


def roll_x(tile):
    out = []
    low = iota((8, 128), 0) < 4
    for p in range(KS):
        b = tile[56 * p:56 * p + 56]

        def by(v, n):
            return v if n == 0 else pltpu.roll(v, n, 1)

        out.append(by(b[0:24], 2 * p))
        out.append(jnp.where(low, by(b[24:32], 2 * p), by(b[24:32], 2 * p + 1)))
        out.append(by(b[32:56], 2 * p + 1))
    return out


def roll_y(tile):
    out = []
    low = iota((8, 128), 0) < 4
    for p in range(KS):
        b = tile[56 * p:56 * p + 56]
        out.append(pltpu.roll(b[0:24], 0, 1, stride=1, stride_axis=0))
        mid = b[24:32]
        first = pltpu.roll(mid, 24, 1, stride=1, stride_axis=0)
        second = pltpu.roll(pltpu.roll(mid, 124, 1), 0, 1, stride=1, stride_axis=0)
        out.append(jnp.where(low, first, second))
        out.append(pltpu.roll(b[32:56], 4, 1, stride=1, stride_axis=0))
    return out


def kernel(
    kc_ref, x_ref, g_ref, wq_ref, wqt_ref, wpt_ref, w1_ref, w1t_ref, w2_ref, w2t_ref,
    relf_ref, relb_ref, vec_ref, pk_ref, pv_ref,
    out_ref, ig_ref, gq_ref, gp_ref, g1_ref, g2_ref, grel_ref, gpk_ref, gpv_ref, gln_ref, tail_ref,
    kvs, gps, gkvs, kf, kb, vx,
):
    step = pl.program_id(0)

    @pl.when(step == 0)
    def _():
        for ref in (gq_ref, gp_ref, g1_ref, g2_ref, grel_ref, gpk_ref, gpv_ref, gln_ref, tail_ref):
            ref[...] = jnp.zeros_like(ref)
        kvs[...] = jnp.zeros_like(kvs)
        gps[...] = jnp.zeros_like(gps)
        key = iota((256, 128), 0)
        lane = iota((256, 128), 1)
        ki = key >> 4
        kj = key & 15
        spot = lane & 63
        low = lane < 64
        real = (kj < KS) & (ki < KS)
        for c, h in [(c, h) for c in range(PAIR) for h in range(HEADS)]:
            first, second = (ki, kj) if h == 0 else (kj, ki)
            which = jnp.where(low, first, second)
            kf[c, h, :, 128:] = jnp.where((spot == 27 + 2 * which) & real, 1.0, 0.0).astype(bf)
            kb[c, h, :, 128:] = jnp.where((spot == 26 - 2 * which) & real, 1.0, 0.0).astype(bf)
            kf[c, h, :, :128] = jnp.where((lane == HD) & (key >= 0), FILL, 0.0).astype(bf)
            kb[c, h, :, :128] = jnp.zeros((256, 128), bf)
            vx[c, h, :, :128] = jnp.zeros((256, 128), bf)
            vx[c, h, :, 128:] = jnp.ones((256, 128), bf)

    steps = [
        canvas(
            step * PAIR + c, c, kc_ref, x_ref, g_ref, wq_ref, wqt_ref, wpt_ref, w1_ref, w1t_ref, w2_ref, w2t_ref,
            relf_ref, relb_ref, vec_ref, pk_ref, pv_ref,
            out_ref, ig_ref, gq_ref, gp_ref, g1_ref, g2_ref, grel_ref, gpk_ref, gpv_ref, gln_ref, tail_ref,
            kvs.at[c], gps.at[c], gkvs.at[c], kf.at[c], kb.at[c], vx.at[c])
        for c in range(PAIR)]
    live = list(steps)
    started = 0
    tick = 0
    while live:
        for c, one in enumerate(steps):
            if one in live and tick >= c * SKEW:
                try:
                    next(one)
                except StopIteration:
                    live.remove(one)
        tick += 1


def canvas(
    item, slot, kc_ref, x_ref, g_ref, wq_ref, wqt_ref, wpt_ref, w1_ref, w1t_ref, w2_ref, w2t_ref,
    relf_ref, relb_ref, vec_ref, pk_ref, pv_ref,
    out_ref, ig_ref, gq_ref, gp_ref, g1_ref, g2_ref, grel_ref, gpk_ref, gpv_ref, gln_ref, tail_ref,
    kvs, gps, gkvs, kf, kb, vx,
):
    lane128 = iota((1, 128), 1)
    mask96 = (lane128 < HD).astype(f32)
    lowhalf = iota((NTOK, 128), 1) < 64

    gain1, shift1, gain2, shift2, fc2_bias = [lanes(vec_ref[n]) for n in range(5)]

    x = x_ref[slot].astype(f32)
    u1, r1 = norm_cols(x)
    nb = with_ones((u1 * gain1 + shift1).astype(bf))
    qb = dot_tn(nb, wq_ref[:, :256]).astype(bf)
    for n in range(4):
        kvs[n, BASE:BASE + NTOK, :] = dot_tn(nb, wq_ref[:, 256 + 128 * n:384 + 128 * n])

    yield
    notfirst = (iota((16, 128), 0) > 0).astype(f32)

    def tap(n, x_row, b):
        v = kvs.at[n][pl.ds(BASE + SIDE * x_row + b - 1, 16, stride=2), :]
        return v * notfirst if b == 0 else v

    u_pool, r_pool = [], []
    for n in range(4):
        w = n // 2
        rows = []
        for i in range(KS):
            acc = None
            for a in range(3):
                for b in range(3):
                    t = tap(n, 2 * i + a - 1, b) * pk_ref[w, 3 * a + b:3 * a + b + 1]
                    acc = t if acc is None else acc + t
            rows.append(acc)
        yield
        u, r = norm_parts(jnp.concatenate(rows, 0), mask96, HD)
        u_pool.append(u)
        r_pool.append(r)
        val = u * pv_ref[w:w + 1] + pv_ref[2 + w:3 + w]
        h = n % 2
        if w == 0:
            val = val * (SCALE * LOG2E)
            kb[h, 0:224, :128] = val.astype(bf)
            pad = ((iota((224, 128), 0) & 15) >= KS) & (iota((224, 128), 1) == HD)
            kf[h, 0:224, :128] = jnp.where(pad, FILL, val).astype(bf)
        else:
            vx[h, 0:224, :128] = val.astype(bf)

    yield
    row_cut = 0
    col_cut = 0
    for n in range(KS):
        row_cut = row_cut + jnp.where(kc_ref[item, KS * n] < 2, 2, 0)
        col_cut = col_cut + jnp.where((kc_ref[item, n] & 1) == 0, 2, 0)
    spot = (lane128 & 63) - 27
    row_side = spot >= row_cut
    col_side = spot >= col_cut
    rows_before = jnp.where(row_side, FILL, 0.0)
    rows_after = jnp.where(row_side, 0.0, FILL)
    y56 = iota((56, 128), 0)
    y56 = jnp.where(y56 >= SIDE, y56 - SIDE, y56)
    col_bias = jnp.where((y56 >= col_cut) != col_side, FILL, 0.0)

    a_h = dot(qb, relf_ref[:, :128])
    a_w = dot(qb, relf_ref[:, 128:])
    pieces_h = roll_x(a_h)
    pieces_w = roll_y(a_w)
    done_h, done_w = [], []
    for p in range(KS):
        row_bias = jnp.where(2 * p >= row_cut, rows_after, rows_before)
        done_h.append(jnp.concatenate(pieces_h[3 * p:3 * p + 3], 0) + row_bias)
        done_w.append(jnp.concatenate(pieces_w[3 * p:3 * p + 3], 0) + col_bias)
    t_h = jnp.concatenate(done_h, 0)
    t_w = jnp.concatenate(done_w, 0)
    rel = (jnp.where(lowhalf, t_h, t_w).astype(bf), jnp.where(lowhalf, t_w, t_h).astype(bf))

    yield
    eb, inv, mixed = [], [], []
    for h in range(HEADS):
        left = jnp.concatenate([qb[:, 128 * h:128 * h + 128], rel[h]], 1)
        s = dot_nt(left, kf[h])
        e = jnp.exp2(s - jnp.max(s, -1, keepdims=True)).astype(bf)
        yield
        o = dot(e, vx[h])
        rinv = 1.0 / o[:, 128:]
        eb.append(e)
        inv.append(rinv)
        mixed.append(o[:, :128] * rinv)
    ab = (jnp.concatenate(mixed, 1) + qb.astype(f32)).astype(bf)

    yield
    middle = x + dot_nt(wpt_ref[...], ab)
    u2, r2 = norm_cols(middle)
    n2b = with_ones((u2 * gain2 + shift2).astype(bf))
    gb = g_ref[slot]
    act, gh = [], []
    for n in range(3):
        cols = slice(256 * n, 256 * n + 256)
        hid = dot_tn(n2b, w1_ref[:, cols])
        phi = 0.5 * lax.erf(hid * 0.7071067811865476) + 0.5
        slope = phi + hid * jnp.exp2(hid * hid * (-0.5 * LOG2E)) * 0.3989422804014327
        yield
        act.append((hid * phi).astype(bf))
        gh.append((dot_tn(gb, w2t_ref[:, cols]) * slope).astype(bf))
    yield
    act = jnp.concatenate(act, 1)
    gh = jnp.concatenate(gh, 1)
    out = middle + fc2_bias + dot_nt(w2t_ref[...], act)
    out_ref[slot] = out.astype(bf)
    g2_ref[...] += dot(gb, act)
    g1_ref[...] += dot(n2b, gh)
    yield
    g = gb.astype(f32)
    add_lanes(gln_ref, tail_ref, 4, g)
    e2 = dot_nt(w1_ref[:D], gh)
    add_lanes(gln_ref, tail_ref, 2, e2 * u2)
    add_lanes(gln_ref, tail_ref, 3, e2)
    gm = g + norm_cols_back(e2 * gain2, u2, r2)
    grb = gm.astype(bf)
    gp_ref[...] += dot(grb, ab)
    yield
    gatt = dot_tn(grb, wpt_ref[...]).astype(bf).astype(f32)
    gr, gcont = [], []
    g2bs, dss = [], []
    for h in range(HEADS):
        ga = gatt[:, 128 * h:128 * h + 128]
        g2b = (ga * (inv[h] * LN2)).astype(bf)
        dd = jnp.sum(g2b.astype(f32) * mixed[h], -1, keepdims=True)
        yield
        gpr = dot_nt(g2b, vx[h, :, :128])
        ds = (eb[h].astype(f32) * (gpr - dd)).astype(bf)
        back = dot(ds, kb[h])
        gcont.append(back[:, :128])
        gr.append(back[:, 128:])
        dss.append(ds)
        g2bs.append(g2b)
    yield
    b_h = jnp.concatenate(roll_x(jnp.where(lowhalf, gr[0], gr[1])), 0)
    b_w = jnp.concatenate(roll_y(jnp.where(lowhalf, gr[1], gr[0])), 0)
    gab = jnp.concatenate([b_h, b_w], 1).astype(bf)
    gq = jnp.concatenate(gcont, 1) + dot(gab, relb_ref[...]) + gatt

    yield
    for n in range(4):
        w, h = n // 2, n % 2
        if w == 0:
            qt = dot_tn(qb[:, 128 * h:128 * h + 128], jnp.concatenate([dss[h], gab], 1))
            grel_ref[128 * h:128 * h + 128] += qt[:, 256:]
            e = jnp.transpose(qt[:, :256])[:224] * (SCALE * LOG2E)
        else:
            e = jnp.transpose(dot_tn(g2bs[h], eb[h]))[:224] * LOG2E
        yield
        gpv_ref[0, n] += fold(e * u_pool[n])
        gpv_ref[1, n] += fold(e)
        gps[n, 0:224, :] = norm_back(e * pv_ref[w:w + 1], u_pool[n], r_pool[n], HD)

    yield
    for n in range(4):
        w = n // 2
        for a in range(3):
            for b in range(3):
                acc = None
                for i in range(KS):
                    t = gps[n, 16 * i:16 * i + 16, :] * tap(n, 2 * i + a - 1, b)
                    acc = t if acc is None else acc + t
                gpk_ref[3 * a + b, n] += acc[0:8] + acc[8:16]

        yield

        def wk(a, b):
            return pk_ref[w, 3 * a + b:3 * a + b + 1]

        for i in range(KS):
            p0 = gps[n, 16 * i:16 * i + 16, :]
            p0s = gps[n, 16 * i + 1:16 * i + 17, :]
            p1 = gps[n, 16 * i + 16:16 * i + 32, :]
            p1s = gps[n, 16 * i + 17:16 * i + 33, :]
            even = SIDE * 2 * i
            odd = even + SIDE
            ee = p0 * wk(1, 1)
            eo = p0 * wk(1, 2) + p0s * wk(1, 0)
            oe = p0 * wk(2, 1) + p1 * wk(0, 1)
            oo = p0 * wk(2, 2) + p0s * wk(2, 0) + p1 * wk(0, 2) + p1s * wk(0, 0)
            gk = gkvs.at[n]
            gk[pl.ds(even, KS, stride=2), :] = ee[:KS]
            gk[pl.ds(even + 1, KS, stride=2), :] = eo[:KS]
            gk[pl.ds(odd, KS, stride=2), :] = oe[:KS]
            gk[pl.ds(odd + 1, KS, stride=2), :] = oo[:KS]

    yield
    gpk = jnp.concatenate([gq.astype(bf)] + [gkvs[n].astype(bf) for n in range(4)], 1)
    gq_ref[...] += dot(nb, gpk)
    e1 = dot_nt(wq_ref[:D], gpk)
    yield
    add_lanes(gln_ref, tail_ref, 0, e1 * u1)
    add_lanes(gln_ref, tail_ref, 1, e1)
    ig_ref[slot] = gm + norm_cols_back(e1 * gain1, u1, r1)


def pad_heads(v, groups):
    lead = v.shape[:-1]
    v = v.reshape(lead + (groups, HD))
    v = jnp.pad(v, ((0, 0),) * len(lead) + ((0, 0), (0, 128 - HD)))
    return v.reshape(lead + (groups * 128,))


def with_bias(weight, bias):
    hi = bias.astype(bf)
    lo = (bias - hi.astype(f32)).astype(bf)
    return jnp.concatenate([weight, hi[None], lo[None], jnp.zeros((14,) + bias.shape, bf)], 0)


def compute(
    block_input, key_crop, first_gain, first_bias, qkv_full, qkv_bias, pool_kernel, pool_gain,
    pool_bias, rel_height, rel_width, proj_full, proj_bias, second_gain, second_bias, fc1_full,
    fc1_bias, fc2_full, fc2_bias, cotangent,
):
    canvases = block_input.shape[0]
    spare = (jnp.arange(256) % 128 == HD).astype(f32)
    wq = with_bias(pad_heads(qkv_full, 6), pad_heads(qkv_bias, 6) + jnp.pad(spare, (0, 512)))
    wqt = pad_heads(qkv_full, 6).T
    proj_hi = proj_bias.astype(bf)
    proj_lo = (proj_bias - proj_hi.astype(f32)).astype(bf)
    wpt = pad_heads(proj_full.T, 2).at[:, HD].set(proj_hi).at[:, 128 + HD].set(proj_lo)
    w1 = with_bias(fc1_full, fc1_bias)
    w1t = fc1_full.T
    w2 = fc2_full
    w2t = fc2_full.T
    rel_h = jnp.pad(rel_height[:54] * LOG2E, ((0, 10), (0, 32)))
    rel_w = jnp.pad(rel_width[:54] * LOG2E, ((0, 10), (0, 32)))
    zero = jnp.zeros((64, 128), f32)
    relb = jnp.concatenate([
        jnp.concatenate([rel_h, zero], 1), jnp.concatenate([zero, rel_h], 1),
        jnp.concatenate([zero, rel_w], 1), jnp.concatenate([rel_w, zero], 1)], 0)
    flip_h = jnp.pad(rel_height[:54][::-1] * LOG2E, ((0, 10), (0, 32)))
    flip_w = jnp.pad(rel_width[:54][::-1] * LOG2E, ((0, 10), (0, 32)))
    relf = jnp.concatenate([
        jnp.concatenate([flip_h, zero], 1), jnp.concatenate([zero, flip_h], 1),
        jnp.concatenate([zero, flip_w], 1), jnp.concatenate([flip_w, zero], 1)], 0).T
    relb = relb.astype(bf)
    relf = relf.astype(bf)
    vec = jnp.broadcast_to(jnp.stack([first_gain, first_bias, second_gain, second_bias, fc2_bias])[..., None], (5, D, 128))
    pk = jnp.pad(pool_kernel, ((0, 0), (0, 0), (0, 32)))
    pv = jnp.pad(jnp.concatenate([pool_gain, pool_bias], 0), ((0, 0), (0, 32)))

    whole = lambda v: pl.BlockSpec(v.shape, lambda i, n=v.ndim: (0,) * n)
    per = lambda: pl.BlockSpec((PAIR, D, NTOK), lambda i: (i, 0, 0))
    consts = (wq, wqt, wpt, w1, w1t, w2, w2t, relf, relb, vec, pk, pv)
    sums = [(208, 768), (D, 256), (208, 768), (D, 768), (256, 256), (9, 4, 8, 128), (2, 4, 8, 128), (5, D, 128), (5, D, 16)]
    results = pl.pallas_call(
        kernel,
        grid=(canvases // PAIR,),
        in_specs=[pl.BlockSpec(memory_space=pltpu.SMEM), per(), per()] + [whole(v) for v in consts],
        out_specs=[per(), per()] + [pl.BlockSpec(s, lambda i, n=len(s): (0,) * n) for s in sums],
        out_shape=[jax.ShapeDtypeStruct((canvases, D, NTOK), bf), jax.ShapeDtypeStruct((canvases, D, NTOK), f32)]
        + [jax.ShapeDtypeStruct(s, f32) for s in sums],
        scratch_shapes=[
            pltpu.VMEM((PAIR, 4, KVROWS, 128), f32),
            pltpu.VMEM((PAIR, 4, 272, 128), f32),
            pltpu.VMEM((PAIR, 4, NTOK, 128), f32),
            pltpu.VMEM((PAIR, 2, 256, 256), bf),
            pltpu.VMEM((PAIR, 2, 256, 256), bf),
            pltpu.VMEM((PAIR, 2, 256, 256), bf),
        ],
        compiler_params=pltpu.CompilerParams(vmem_limit_bytes=60 * 2**20),
        name="block_step",
    )(key_crop, jnp.swapaxes(block_input, 1, 2), jnp.swapaxes(cotangent, 1, 2), *consts)
    out, ig, gq, gp, g1, g2, grel, gpk, gpv, gln, tail = results
    out = jnp.swapaxes(out, 1, 2)
    ig = jnp.swapaxes(ig, 1, 2)

    def unpad(v, groups):
        lead = v.shape[:-1]
        return v.reshape(lead + (groups, 128))[..., :HD].reshape(lead + (groups * HD,))

    gq_full = unpad(gq, 6)
    grad_qkv_weight, grad_qkv_bias = gq_full[:D], gq_full[D]
    grad_proj_weight = unpad(gp, 2).T
    grad_proj_bias = gp[:, HD]
    grad_fc1_weight, grad_fc1_bias = g1[:D], g1[D]
    grad_fc2_weight = g2.T
    h0, h1 = grel[:HD], grel[128:128 + HD]
    rel_pad = lambda v: jnp.pad(v.T[:54], ((0, 1), (0, 0))) * LOG2E
    grad_rel_height = rel_pad(h0[:, 0:64] + h1[:, 64:128])
    grad_rel_width = rel_pad(h0[:, 192:256] + h1[:, 128:192])
    gpk = gpk.sum(2)[..., :HD]
    grad_pool_kernel = jnp.stack([gpk[:, 0] + gpk[:, 1], gpk[:, 2] + gpk[:, 3]])
    gpv = gpv.sum(2)[..., :HD]
    grad_pool_gain = jnp.stack([gpv[0, 0] + gpv[0, 1], gpv[0, 2] + gpv[0, 3]])
    grad_pool_bias = jnp.stack([gpv[1, 0] + gpv[1, 1], gpv[1, 2] + gpv[1, 3]])
    gln = gln.sum(2) + tail.sum(2)
    return dict(
        out=out, ig=ig, qkv=grad_qkv_weight, proj=grad_proj_weight, fc1=grad_fc1_weight, fc2=grad_fc2_weight,
        small=(gln[0], gln[1], grad_qkv_bias, grad_pool_kernel, grad_pool_gain, grad_pool_bias,
               grad_rel_height, grad_rel_width, grad_proj_bias, gln[2], gln[3], grad_fc1_bias, gln[4]))


def gather_weights(shards):
    flat = jnp.concatenate([v.T.reshape(-1) for v in shards])
    every = lax.all_gather(flat, ("dp", "fsdp"), axis=0, tiled=False)
    dp, fsdp = lax.axis_size("dp"), lax.axis_size("fsdp")
    full = []
    start = 0
    for v in shards:
        rows, cols = v.shape
        part = every[:, start:start + rows * cols].reshape(dp, fsdp, cols, rows)
        full.append(jnp.transpose(part, (1, 3, 0, 2)).reshape(fsdp * rows, dp * cols))
        start += rows * cols
    return full


def reduce_weights(grads, shards):
    dp, fsdp = lax.axis_size("dp"), lax.axis_size("fsdp")
    parts = []
    for grad, v in zip(grads, shards):
        rows, cols = v.shape
        part = jnp.transpose(grad.astype(bf).reshape(fsdp, rows, dp, cols), (2, 0, 3, 1))
        parts.append(part.reshape(dp * fsdp, cols * rows))
    flat = jnp.concatenate(parts, 1)
    mine = lax.psum_scatter(flat, ("dp", "fsdp"), scatter_dimension=0, tiled=False).astype(f32)
    owned = []
    start = 0
    for v in shards:
        rows, cols = v.shape
        owned.append(mine[start:start + rows * cols].reshape(cols, rows).T)
        start += rows * cols
    return owned


def local(
    block_input, token_crop, key_crop, first_gain, first_bias, qkv_weight, qkv_bias, pool_kernel, pool_gain,
    pool_bias, rel_height, rel_width, proj_weight, proj_bias, second_gain, second_bias, fc1_weight, fc1_bias,
    fc2_weight, fc2_bias, cotangent,
):
    shards = (qkv_weight, proj_weight, fc1_weight, fc2_weight)
    qkv_full, proj_full, fc1_full, fc2_full = gather_weights(shards)
    r = compute(
        block_input, key_crop, first_gain, first_bias, qkv_full, qkv_bias, pool_kernel, pool_gain, pool_bias,
        rel_height, rel_width, proj_full, proj_bias, second_gain, second_bias, fc1_full, fc1_bias, fc2_full,
        fc2_bias, cotangent)
    owned = reduce_weights((r["qkv"], r["proj"], r["fc1"], r["fc2"]), shards)
    small = r["small"]
    flat = jnp.concatenate([v.reshape(-1) for v in small])
    flat = lax.psum(flat, ("dp", "fsdp"))
    summed = []
    start = 0
    for v in small:
        summed.append(flat[start:start + v.size].reshape(v.shape))
        start += v.size
    return (
        r["out"], r["ig"], summed[0], summed[1], owned[0], summed[2], summed[3], summed[4], summed[5], summed[6],
        summed[7], owned[1], summed[8], summed[9], summed[10], owned[2], summed[11], owned[3], summed[12])


def solution(mesh):
    rows = P(("dp", "fsdp"), None, None)
    ids = P(("dp", "fsdp"), None)
    block = P("fsdp", "dp")
    one = P()
    return jax.shard_map(
        local,
        mesh=mesh,
        in_specs=(rows, ids, ids, one, one, block, one, one, one, one, one, one, block, one, one, one, block, one,
                  block, one, rows),
        out_specs=(rows, rows, one, one, block, one, one, one, one, one, one, block, one, one, one, block, one,
                   block, one),
        check_vma=False,
    )
```

```python
import functools

import jax
import jax.numpy as jnp
from jax import lax
from jax.experimental import pallas as pl
from jax.experimental.pallas import tpu as pltpu
from jax.sharding import PartitionSpec as P

D = 192
HEADS = 2
HD = 96
FF = 768
SIDE = 28
KS = 14
NTOK = 784
NKEY = 196
REL = 55

EPS = 1e-06
FILL = -1e30
LOG2E = 1.4426950408889634
LN2 = 0.6931471805599453
SCALE = HD ** (-0.5)
BASE = 32
KVROWS = BASE + NTOK + 24
bf = jnp.bfloat16
PAIR = 2
SKEW = 3
FEAT = 208
f32 = jnp.float32


def dot(a, b):
    return jnp.dot(a, b, preferred_element_type=f32)


def dot_nt(a, b):
    return lax.dot_general(a, b, (((1,), (1,)), ((), ())), preferred_element_type=f32)


def dot_tn(a, b):
    return lax.dot_general(a, b, (((0,), (0,)), ((), ())), preferred_element_type=f32)


def iota(shape, dim):
    return lax.broadcasted_iota(jnp.int32, shape, dim)


def widen(v):
    return jnp.concatenate([v, jnp.zeros((v.shape[0], 256 - v.shape[1]), v.dtype)], axis=1)


def lanes(col):
    return jnp.concatenate([col] * 6 + [col[:, :16]], axis=1)


def fold_lanes(v):
    total = v[:, 0:128]
    for n in range(1, 6):
        total = total + v[:, 128 * n:128 * n + 128]
    return total


def add_lanes(ref, tail, n, v):
    ref[n] += fold_lanes(v)
    tail[n] += v[:, 768:784]


def with_ones(v):
    extra = (iota((16, NTOK), 0) < 2).astype(f32).astype(bf)
    return jnp.concatenate([v, extra], 0)


def norm_cols(v):
    mean = jnp.sum(v, 0, keepdims=True) * (1.0 / D)
    c = v - mean
    var = jnp.sum(c * c, 0, keepdims=True) * (1.0 / D)
    r = lax.rsqrt(var + EPS)
    return c * r, r


def norm_cols_back(ge, u, r):
    s1 = jnp.sum(ge, 0, keepdims=True) * (1.0 / D)
    s2 = jnp.sum(ge * u, 0, keepdims=True) * (1.0 / D)
    return (ge - s1 - u * s2) * r


def fold(v):
    total = v[0:8]
    for n in range(1, v.shape[0] // 8):
        total = total + v[8 * n:8 * n + 8]
    return total


def norm_parts(v, mask, width):
    mean = jnp.sum(v, -1, keepdims=True) * (1.0 / width)
    c = (v - mean) * mask
    var = jnp.sum(c * c, -1, keepdims=True) * (1.0 / width)
    r = lax.rsqrt(var + EPS)
    return c * r, r


def norm_back(ge, u, r, width):
    s1 = jnp.sum(ge, -1, keepdims=True) * (1.0 / width)
    s2 = jnp.sum(ge * u, -1, keepdims=True) * (1.0 / width)
    return (ge - s1 - u * s2) * r


def roll_x(tile):
    out = []
    low = iota((8, 128), 0) < 4
    for p in range(KS):
        b = tile[56 * p:56 * p + 56]

        def by(v, n):
            return v if n == 0 else pltpu.roll(v, n, 1)

        out.append(by(b[0:24], 2 * p))
        out.append(jnp.where(low, by(b[24:32], 2 * p), by(b[24:32], 2 * p + 1)))
        out.append(by(b[32:56], 2 * p + 1))
    return out


def roll_y(tile):
    out = []
    low = iota((8, 128), 0) < 4
    for p in range(KS):
        b = tile[56 * p:56 * p + 56]
        out.append(pltpu.roll(b[0:24], 0, 1, stride=1, stride_axis=0))
        mid = b[24:32]
        first = pltpu.roll(mid, 24, 1, stride=1, stride_axis=0)
        second = pltpu.roll(pltpu.roll(mid, 124, 1), 0, 1, stride=1, stride_axis=0)
        out.append(jnp.where(low, first, second))
        out.append(pltpu.roll(b[32:56], 4, 1, stride=1, stride_axis=0))
    return out


def kernel(
    wire, kc_ref, x_ref, g_ref, wq_ref, wpt_ref, w1_ref, w2t_ref,
    relf_ref, relb_ref, vec_ref, pk_ref, pv_ref,
    out_ref, ig_ref, wire_ref, small_ref,
    gq_ref, gp_ref, g1_ref, g2_ref, grel_ref, gpk_ref, gpv_ref, gln_ref, tail_ref, table, piece,
    kvs, gps, gkvs, kf, kb, vx,
):
    step = pl.program_id(0)

    @pl.when(step == 0)
    def _():
        for ref in (gq_ref, gp_ref, g1_ref, g2_ref, grel_ref, gpk_ref, gpv_ref, gln_ref, tail_ref):
            ref[...] = jnp.zeros_like(ref)
        kvs[...] = jnp.zeros_like(kvs)
        gps[...] = jnp.zeros_like(gps)
        key = iota((256, 128), 0)
        lane = iota((256, 128), 1)
        ki = key >> 4
        kj = key & 15
        spot = lane & 63
        low = lane < 64
        real = (kj < KS) & (ki < KS)
        for c, h in [(c, h) for c in range(PAIR) for h in range(HEADS)]:
            first, second = (ki, kj) if h == 0 else (kj, ki)
            which = jnp.where(low, first, second)
            kf[c, h, :, 128:] = jnp.where((spot == 27 + 2 * which) & real, 1.0, 0.0).astype(bf)
            kb[c, h, :, 128:] = jnp.where((spot == 26 - 2 * which) & real, 1.0, 0.0).astype(bf)
            kf[c, h, :, :128] = jnp.where((lane == HD) & (key >= 0), FILL, 0.0).astype(bf)
            kb[c, h, :, :128] = jnp.zeros((256, 128), bf)
            vx[c, h, :, :128] = jnp.zeros((256, 128), bf)
            vx[c, h, :, 128:] = jnp.ones((256, 128), bf)

    steps = [
        canvas(
            step * PAIR + c, c, kc_ref, x_ref, g_ref, wq_ref, wpt_ref, w1_ref, w2t_ref,
            relf_ref, relb_ref, vec_ref, pk_ref, pv_ref,
            out_ref, ig_ref, gq_ref, gp_ref, g1_ref, g2_ref, grel_ref, gpk_ref, gpv_ref, gln_ref, tail_ref,
            kvs.at[c], gps.at[c], gkvs.at[c], kf.at[c], kb.at[c], vx.at[c])
        for c in range(PAIR)]
    live = list(steps)
    started = 0
    tick = 0
    while live:
        for c, one in enumerate(steps):
            if one in live and tick >= c * SKEW:
                try:
                    next(one)
                except StopIteration:
                    live.remove(one)
        tick += 1

    @pl.when(step == pl.num_programs(0) - 1)
    def _():
        pack(wire, wire_ref, small_ref, gq_ref, gp_ref, g1_ref, g2_ref, grel_ref, gpk_ref, gpv_ref, gln_ref,
             tail_ref, table, piece)


def pack(wire, wire_ref, small_ref, gq_ref, gp_ref, g1_ref, g2_ref, grel_ref, gpk_ref, gpv_ref, gln_ref, tail_ref,
         table, piece):
    wide = wire.width
    for g in range(6):
        table[HD * g:HD * g + HD, :] = jnp.transpose(gq_ref[:D, 128 * g:128 * g + 128])[:HD]
    table[3 * D:4 * D, :] = jnp.concatenate([gp_ref[:, 0:HD], gp_ref[:, 128:128 + HD]], 1)
    table[4 * D:4 * D + FF, :] = jnp.transpose(g1_ref[:D])
    piece[...] = jnp.zeros_like(piece)
    for d in range(wire.dp):
        for first, count, at in wire.starts(d):
            piece[first:first + count, :] = table[at:at + count, :]
        low = g2_ref[wire.low * d:wire.low * (d + 1), :]
        for f in range(wire.fsdp):
            for q in range(wire.parts):
                first = wire.top + q * wire.low
                at = (f * wire.parts + q) * wide
                piece[first:first + wire.low, f * wide:(f + 1) * wide] = low[:, at:at + wide]
        for f in range(wire.fsdp):
            part = piece[:, f * wide:(f + 1) * wide]
            part = jnp.concatenate([part, jnp.zeros((wire.pad, 128 - wide), f32)], 1)
            wire_ref[wire.slot(d, f)] = part.astype(bf)
    small_ref[...] = jnp.zeros_like(small_ref)
    turned = jnp.transpose(grel_ref[...]) * LOG2E
    small_ref[0:64] = turned[0:64, 0:128] + turned[64:128, 128:256]
    small_ref[64:128] = turned[192:256, 0:128] + turned[128:192, 128:256]
    for w in range(2):
        for k in range(9):
            small_ref[128 + 9 * w + k:129 + 9 * w + k] = jnp.sum(
                gpk_ref[k, 2 * w] + gpk_ref[k, 2 * w + 1], 0, keepdims=True)
        for m in range(2):
            small_ref[146 + 2 * m + w:147 + 2 * m + w] = jnp.sum(
                gpv_ref[m, 2 * w] + gpv_ref[m, 2 * w + 1], 0, keepdims=True)
    for g in range(6):
        small_ref[152 + g:153 + g] = gq_ref[D:D + 1, 128 * g:128 * g + 128]
        small_ref[158 + g:159 + g] = g1_ref[D:D + 1, 128 * g:128 * g + 128]
    rows = []
    for k in range(5):
        rows.append(jnp.sum(jnp.transpose(gln_ref[k]), 0, keepdims=True)
                    + jnp.sum(jnp.transpose(tail_ref[k]), 0, keepdims=True))
    rows.append(jnp.transpose(gp_ref[:, 0:128])[HD:HD + 1])
    for k, v in enumerate(rows):
        small_ref[164 + 2 * k:165 + 2 * k] = v[:, 0:128]
        small_ref[165 + 2 * k:166 + 2 * k] = jnp.concatenate([v[:, 128:D], jnp.zeros((1, 256 - D), f32)], 1)


def canvas(
    item, slot, kc_ref, x_ref, g_ref, wq_ref, wpt_ref, w1_ref, w2t_ref,
    relf_ref, relb_ref, vec_ref, pk_ref, pv_ref,
    out_ref, ig_ref, gq_ref, gp_ref, g1_ref, g2_ref, grel_ref, gpk_ref, gpv_ref, gln_ref, tail_ref,
    kvs, gps, gkvs, kf, kb, vx,
):
    lane128 = iota((1, 128), 1)
    mask96 = (lane128 < HD).astype(f32)
    lowhalf = iota((NTOK, 128), 1) < 64

    gain1, shift1, gain2, shift2, fc2_bias = [lanes(vec_ref[n]) for n in range(5)]

    x = x_ref[slot].astype(f32)
    u1, r1 = norm_cols(x)
    nb = with_ones((u1 * gain1 + shift1).astype(bf))
    qb = dot_tn(nb, wq_ref[:, :256]).astype(bf)
    for n in range(4):
        kvs[n, BASE:BASE + NTOK, :] = dot_tn(nb, wq_ref[:, 256 + 128 * n:384 + 128 * n])

    yield
    notfirst = (iota((16, 128), 0) > 0).astype(f32)

    def tap(n, x_row, b):
        v = kvs.at[n][pl.ds(BASE + SIDE * x_row + b - 1, 16, stride=2), :]
        return v * notfirst if b == 0 else v

    u_pool, r_pool = [], []
    for n in range(4):
        w = n // 2
        rows = []
        for i in range(KS):
            acc = None
            for a in range(3):
                for b in range(3):
                    t = tap(n, 2 * i + a - 1, b) * pk_ref[w, 3 * a + b:3 * a + b + 1]
                    acc = t if acc is None else acc + t
            rows.append(acc)
        yield
        u, r = norm_parts(jnp.concatenate(rows, 0), mask96, HD)
        u_pool.append(u)
        r_pool.append(r)
        val = u * pv_ref[w:w + 1] + pv_ref[2 + w:3 + w]
        h = n % 2
        if w == 0:
            val = val * (SCALE * LOG2E)
            kb[h, 0:224, :128] = val.astype(bf)
            pad = ((iota((224, 128), 0) & 15) >= KS) & (iota((224, 128), 1) == HD)
            kf[h, 0:224, :128] = jnp.where(pad, FILL, val).astype(bf)
        else:
            vx[h, 0:224, :128] = val.astype(bf)

    yield
    row_cut = 0
    col_cut = 0
    for n in range(KS):
        row_cut = row_cut + jnp.where(kc_ref[item, KS * n] < 2, 2, 0)
        col_cut = col_cut + jnp.where((kc_ref[item, n] & 1) == 0, 2, 0)
    spot = (lane128 & 63) - 27
    row_side = spot >= row_cut
    col_side = spot >= col_cut
    rows_before = jnp.where(row_side, FILL, 0.0)
    rows_after = jnp.where(row_side, 0.0, FILL)
    y56 = iota((56, 128), 0)
    y56 = jnp.where(y56 >= SIDE, y56 - SIDE, y56)
    col_bias = jnp.where((y56 >= col_cut) != col_side, FILL, 0.0)

    a_h = dot(qb, relf_ref[:, :128])
    a_w = dot(qb, relf_ref[:, 128:])
    pieces_h = roll_x(a_h)
    pieces_w = roll_y(a_w)
    done_h, done_w = [], []
    for p in range(KS):
        row_bias = jnp.where(2 * p >= row_cut, rows_after, rows_before)
        done_h.append(jnp.concatenate(pieces_h[3 * p:3 * p + 3], 0) + row_bias)
        done_w.append(jnp.concatenate(pieces_w[3 * p:3 * p + 3], 0) + col_bias)
    t_h = jnp.concatenate(done_h, 0)
    t_w = jnp.concatenate(done_w, 0)
    rel = (jnp.where(lowhalf, t_h, t_w).astype(bf), jnp.where(lowhalf, t_w, t_h).astype(bf))

    yield
    eb, inv, mixed = [], [], []
    for h in range(HEADS):
        left = jnp.concatenate([qb[:, 128 * h:128 * h + 128], rel[h]], 1)
        s = dot_nt(left, kf[h])
        e = jnp.exp2(s - jnp.max(s, -1, keepdims=True)).astype(bf)
        yield
        o = dot(e, vx[h])
        rinv = 1.0 / o[:, 128:]
        eb.append(e)
        inv.append(rinv)
        mixed.append(o[:, :128] * rinv)
    ab = (jnp.concatenate(mixed, 1) + qb.astype(f32)).astype(bf)

    yield
    middle = x + dot_nt(wpt_ref[...], ab)
    u2, r2 = norm_cols(middle)
    n2b = with_ones((u2 * gain2 + shift2).astype(bf))
    gb = g_ref[slot]
    act, gh = [], []
    for n in range(3):
        cols = slice(256 * n, 256 * n + 256)
        hid = dot_tn(n2b, w1_ref[:, cols])
        phi = 0.5 * lax.erf(hid * 0.7071067811865476) + 0.5
        slope = phi + hid * jnp.exp2(hid * hid * (-0.5 * LOG2E)) * 0.3989422804014327
        yield
        act.append((hid * phi).astype(bf))
        gh.append((dot_tn(gb, w2t_ref[:, cols]) * slope).astype(bf))
    yield
    act = jnp.concatenate(act, 1)
    gh = jnp.concatenate(gh, 1)
    out = middle + fc2_bias + dot_nt(w2t_ref[...], act)
    out_ref[slot] = out.astype(bf)
    g2_ref[...] += dot(gb, act)
    g1_ref[...] += dot(n2b, gh)
    yield
    g = gb.astype(f32)
    add_lanes(gln_ref, tail_ref, 4, g)
    e2 = dot_nt(w1_ref[:D], gh)
    add_lanes(gln_ref, tail_ref, 2, e2 * u2)
    add_lanes(gln_ref, tail_ref, 3, e2)
    gm = g + norm_cols_back(e2 * gain2, u2, r2)
    grb = gm.astype(bf)
    gp_ref[...] += dot(grb, ab)
    yield
    gatt = dot_tn(grb, wpt_ref[...]).astype(bf).astype(f32)
    gr, gcont = [], []
    g2bs, dss = [], []
    for h in range(HEADS):
        ga = gatt[:, 128 * h:128 * h + 128]
        g2b = (ga * (inv[h] * LN2)).astype(bf)
        dd = jnp.sum(g2b.astype(f32) * mixed[h], -1, keepdims=True)
        yield
        gpr = dot_nt(g2b, vx[h, :, :128])
        ds = (eb[h].astype(f32) * (gpr - dd)).astype(bf)
        back = dot(ds, kb[h])
        gcont.append(back[:, :128])
        gr.append(back[:, 128:])
        dss.append(ds)
        g2bs.append(g2b)
    yield
    b_h = jnp.concatenate(roll_x(jnp.where(lowhalf, gr[0], gr[1])), 0)
    b_w = jnp.concatenate(roll_y(jnp.where(lowhalf, gr[1], gr[0])), 0)
    gab = jnp.concatenate([b_h, b_w], 1).astype(bf)
    gq = jnp.concatenate(gcont, 1) + dot(gab, relb_ref[...]) + gatt

    yield
    for n in range(4):
        w, h = n // 2, n % 2
        if w == 0:
            qt = dot_tn(qb[:, 128 * h:128 * h + 128], jnp.concatenate([dss[h], gab], 1))
            grel_ref[128 * h:128 * h + 128] += qt[:, 256:]
            e = jnp.transpose(qt[:, :256])[:224] * (SCALE * LOG2E)
        else:
            e = jnp.transpose(dot_tn(g2bs[h], eb[h]))[:224] * LOG2E
        yield
        gpv_ref[0, n] += fold(e * u_pool[n])
        gpv_ref[1, n] += fold(e)
        gps[n, 0:224, :] = norm_back(e * pv_ref[w:w + 1], u_pool[n], r_pool[n], HD)

    yield
    for n in range(4):
        w = n // 2
        for a in range(3):
            for b in range(3):
                acc = None
                for i in range(KS):
                    t = gps[n, 16 * i:16 * i + 16, :] * tap(n, 2 * i + a - 1, b)
                    acc = t if acc is None else acc + t
                gpk_ref[3 * a + b, n] += acc[0:8] + acc[8:16]

        yield

        def wk(a, b):
            return pk_ref[w, 3 * a + b:3 * a + b + 1]

        for i in range(KS):
            p0 = gps[n, 16 * i:16 * i + 16, :]
            p0s = gps[n, 16 * i + 1:16 * i + 17, :]
            p1 = gps[n, 16 * i + 16:16 * i + 32, :]
            p1s = gps[n, 16 * i + 17:16 * i + 33, :]
            even = SIDE * 2 * i
            odd = even + SIDE
            ee = p0 * wk(1, 1)
            eo = p0 * wk(1, 2) + p0s * wk(1, 0)
            oe = p0 * wk(2, 1) + p1 * wk(0, 1)
            oo = p0 * wk(2, 2) + p0s * wk(2, 0) + p1 * wk(0, 2) + p1s * wk(0, 0)
            gk = gkvs.at[n]
            gk[pl.ds(even, KS, stride=2), :] = ee[:KS]
            gk[pl.ds(even + 1, KS, stride=2), :] = eo[:KS]
            gk[pl.ds(odd, KS, stride=2), :] = oe[:KS]
            gk[pl.ds(odd + 1, KS, stride=2), :] = oo[:KS]

    yield
    gpk = jnp.concatenate([gq.astype(bf)] + [gkvs[n].astype(bf) for n in range(4)], 1)
    gq_ref[...] += dot(nb, gpk)
    e1 = dot_nt(wq_ref[:D], gpk)
    yield
    add_lanes(gln_ref, tail_ref, 0, e1 * u1)
    add_lanes(gln_ref, tail_ref, 1, e1)
    ig_ref[slot] = gm + norm_cols_back(e1 * gain1, u1, r1)


MESH = pl.DeviceIdType.MESH


class Wire:
    def __init__(self, dp, fsdp):
        self.dp, self.fsdp, self.n = dp, fsdp, dp * fsdp
        self.chips = self.n // 2
        self.rows = (3 * D // dp, D // dp, FF // dp)
        self.top = sum(self.rows)
        self.low = D // dp
        self.width = D // fsdp
        self.parts = FF // fsdp // self.width
        self.used = self.top + self.parts * self.low
        self.pad = -(-self.used // 16) * 16

    def starts(self, d):
        a, b, c = self.rows
        return ((0, a, a * d), (a, b, 3 * D + b * d), (a + b, c, 4 * D + c * d))

    def slot(self, d, f):
        return (d % 2) * self.chips + (d // 2) * self.fsdp + f

    def place(self):
        d, f = lax.axis_index("dp"), lax.axis_index("fsdp")
        core = lax.rem(d, 2)
        return core, (d // 2) * self.fsdp + f

    def device(self, core, chip):
        return (2 * (chip // self.fsdp) + core, lax.rem(chip, self.fsdp))


def gather_kernel(
    wire, qkv, proj, fc1, fc2, qkv_bias, proj_bias, fc1_bias, gain1, shift1, gain2, shift2, fc2_bias,
    pool_kernel, pool_gain, pool_bias, rel_h, rel_w,
    wq_ref, wpt_ref, w1_ref, w2t_ref, relf_ref, relb_ref, vec_ref, pk_ref, pv_ref,
    buf, mine, tmp, table, low_table, send, forward, recv,
):
    n, nc = wire.n, wire.chips
    core, chip = wire.place()
    other = 1 - core
    partner = wire.device(other, chip)
    me = core * nc + chip
    barrier = pltpu.get_barrier_semaphore()
    pl.semaphore_signal(barrier, inc=1, device_id=partner, device_id_type=MESH)

    def greet(k, c):
        pl.semaphore_signal(barrier, inc=1, device_id=wire.device(core, lax.rem(chip + k, nc)), device_id_type=MESH)
        return c

    lax.fori_loop(1, nc, greet, 0)

    wide = wire.width
    a, b, c = wire.rows
    tmp[...] = jnp.zeros_like(tmp)
    tmp[0:a, :wide] = qkv[...].astype(f32)
    tmp[a:a + b, :wide] = proj[...].astype(f32)
    tmp[a + b:wire.top, :wide] = fc1[...].astype(f32)
    below = fc2[...].astype(f32)
    for q in range(wire.parts):
        first = wire.top + q * wire.low
        tmp[first:first + wire.low, :wide] = below[:, q * wide:(q + 1) * wide]
    mine[...] = tmp[:, :128].astype(bf)
    pl.semaphore_wait(barrier, nc)

    def to_partner(src, slot, k):
        return pltpu.make_async_remote_copy(
            src_ref=src, dst_ref=buf.at[slot], send_sem=forward.at[k], recv_sem=recv.at[slot],
            device_id=partner, device_id_type=MESH)

    def to_chip(k):
        return pltpu.make_async_remote_copy(
            src_ref=mine, dst_ref=buf.at[me], send_sem=send.at[k], recv_sem=recv.at[me],
            device_id=wire.device(core, lax.rem(chip + k, nc)), device_id_type=MESH)

    def start(k, c):
        to_chip(nc - k).start()
        return c

    lax.fori_loop(1, nc, start, 0)
    to_partner(mine, me, 0).start()

    def row(ref):
        return ref[...].reshape(1, ref.shape[0])

    for k, ref in enumerate((gain1, shift1, gain2, shift2, fc2_bias)):
        vec_ref[k] = jnp.transpose(jnp.broadcast_to(row(ref), (128, D)))
    zero32 = jnp.zeros((64, 128 - HD), f32)

    def tall(ref):
        t = jnp.concatenate([ref[...] * LOG2E, jnp.zeros((64 - REL, HD), f32)], 0)
        t = jnp.concatenate([t, zero32], 1)
        return jnp.where(iota((64, 128), 0) < 54, t, 0.0)

    th, tw = tall(rel_h), tall(rel_w)
    none = jnp.zeros((64, 128), f32)
    relb = jnp.concatenate([
        jnp.concatenate([th, none], 1), jnp.concatenate([none, th], 1),
        jnp.concatenate([none, tw], 1), jnp.concatenate([tw, none], 1)], 0).astype(bf)
    relb_ref[...] = relb
    at, to = iota((256, 256), 0), iota((256, 256), 1)
    mirror = ((at >> 6) == (to >> 6)) & ((at & 63) + (to & 63) == 53)
    relf_ref[...] = dot_tn(relb, jnp.where(mirror, 1.0, 0.0).astype(bf)).astype(bf)
    for w in range(2):
        taps = jnp.concatenate([pool_kernel[k, w:w + 1, :] for k in range(9)], 0)
        pk_ref[w] = jnp.concatenate([taps, jnp.zeros((9, 128 - HD), f32)], 1)
    four = jnp.concatenate([pool_gain[...], pool_bias[...]], 0)
    pv_ref[...] = jnp.concatenate([four, jnp.zeros((4, 128 - HD), f32)], 1)

    def relay(k, c):
        slot = core * nc + lax.rem(chip + k, nc)
        pltpu.make_async_remote_copy(
            src_ref=mine, dst_ref=buf.at[slot], send_sem=send.at[0], recv_sem=recv.at[slot],
            device_id=partner, device_id_type=MESH).wait_recv()
        to_partner(buf.at[slot], slot, k).start()
        return c

    lax.fori_loop(1, nc, relay, 0)

    def arrive(k, c):
        to_partner(mine, other * nc + k, 0).wait_recv()
        return c

    lax.fori_loop(0, nc, arrive, 0)
    buf[pl.ds(me, 1)] = mine[...][None]

    for d in range(wire.dp):
        blocks = [buf[wire.slot(d, f)].astype(f32) for f in range(wire.fsdp)]
        tmp[...] = jnp.concatenate([v[:, :wide] for v in blocks], 1)
        for first, count, to_row in wire.starts(d):
            table[to_row:to_row + count, :] = tmp[first:first + count, :]
        for f in range(wire.fsdp):
            parts = [tmp[wire.top + q * wire.low:wire.top + (q + 1) * wire.low, f * wide:(f + 1) * wide]
                     for q in range(wire.parts)]
            low_table[wire.low * d:wire.low * (d + 1), f * wide * wire.parts:(f + 1) * wide * wire.parts] = (
                jnp.concatenate(parts, 1))

    def two(bias):
        hi = bias.astype(bf).astype(f32)
        return jnp.concatenate([hi, bias - hi, jnp.zeros((14, bias.shape[1]), f32)], 0)

    qb = row(qkv_bias)
    for g in range(6):
        block = jnp.concatenate([jnp.transpose(table[HD * g:HD * g + HD, :]), two(qb[:, HD * g:HD * g + HD])], 0)
        spare = (iota((FEAT, 128 - HD), 0) == D) & (iota((FEAT, 128 - HD), 1) == 0) & (g < 2)
        block = jnp.concatenate([block, jnp.where(spare, 1.0, 0.0)], 1)
        wq_ref[:, 128 * g:128 * g + 128] = block.astype(bf)
    cols = []
    pb = row(proj_bias)
    hi = pb.astype(bf).astype(f32)
    for g, extra in enumerate((hi, pb - hi)):
        col = jnp.transpose(jnp.broadcast_to(extra, (128, D)))[:, :128 - HD]
        col = jnp.where(iota((D, 128 - HD), 1) == 0, col, 0.0)
        cols += [table[3 * D:4 * D, HD * g:HD * g + HD], col]
    wpt_ref[...] = jnp.concatenate(cols, 1).astype(bf)
    w1_ref[...] = jnp.concatenate([jnp.transpose(table[4 * D:4 * D + FF, :]), two(row(fc1_bias))], 0).astype(bf)
    w2t_ref[...] = low_table[...].astype(bf)

    def finish(k, c):
        to_chip(k).wait_send()
        to_partner(mine, me, k).wait_send()
        return c

    lax.fori_loop(1, nc, finish, 0)
    to_partner(mine, me, 0).wait_send()


def staged(body, ins, outs, *refs):
    a, b = len(ins), len(outs)
    src, dst = refs[:a], refs[a:a + b]
    vin, vout = refs[a + b:2 * a + b], refs[2 * a + b:2 * (a + b)]
    sems, rest = refs[2 * (a + b)], refs[2 * (a + b) + 1:]
    loads = [pltpu.make_async_copy(s, v, sems.at[k]) for k, (s, v) in enumerate(zip(src, vin))]
    for c in loads:
        c.start()
    for c in loads:
        c.wait()
    body(*vin, *vout, *rest)
    stores = [pltpu.make_async_copy(v, d, sems.at[k]) for k, (v, d) in enumerate(zip(vout, dst))]
    for c in stores:
        c.start()
    for c in stores:
        c.wait()


def staged_call(body, args, shapes, scratch, **params):
    hbm = pl.BlockSpec(memory_space=pltpu.HBM)
    ins = [(v.shape, v.dtype) for v in args]
    name = params.pop("name")
    return pl.pallas_call(
        functools.partial(staged, body, ins, shapes),
        in_specs=[hbm] * len(ins),
        out_specs=[hbm] * len(shapes),
        out_shape=[jax.ShapeDtypeStruct(*s) for s in shapes],
        scratch_shapes=[pltpu.VMEM(*s) for s in ins + list(shapes)]
        + [pltpu.SemaphoreType.DMA((max(len(ins), len(shapes)),))] + list(scratch),
        compiler_params=pltpu.CompilerParams(**params),
        name=name,
    )(*args)


def gather(wire, shards, vectors):
    shapes = [((FEAT, FF), bf), ((D, 256), bf), ((FEAT, FF), bf), ((D, FF), bf), ((256, 256), bf), ((256, 256), bf),
              ((5, D, 128), f32), ((2, 9, 128), f32), ((4, 128), f32)]
    args = [v.T for v in shards] + list(vectors)
    scratch = [
        pltpu.VMEM((wire.n, wire.pad, 128), bf),
        pltpu.VMEM((wire.pad, 128), bf),
        pltpu.VMEM((wire.pad, D), f32),
        pltpu.VMEM((4 * D + FF, D), f32),
        pltpu.VMEM((D, FF), f32),
        pltpu.SemaphoreType.DMA((wire.chips,)),
        pltpu.SemaphoreType.DMA((wire.chips,)),
        pltpu.SemaphoreType.DMA((wire.n,)),
    ]
    return staged_call(
        functools.partial(gather_kernel, wire), args, shapes, scratch,
        vmem_limit_bytes=60 * 2**20, collective_id=0, has_side_effects=True, name="gather_weights")


def reduce_kernel(
    wire, grads, small, res_ref, sum_ref,
    abuf, comb, bbuf, sbuf, own, gsm, asend, arecv, bsend, brecv, ssend, srecv, gsend, grecv,
):
    n, nc = wire.n, wire.chips
    core, chip = wire.place()
    other = 1 - core
    partner = wire.device(other, chip)
    me = core * nc + chip
    barrier = pltpu.get_barrier_semaphore()

    def peer(k):
        slot = lax.rem(me + k, n)
        return slot, wire.device(slot // nc, lax.rem(slot, nc))

    def greet(k, c):
        pl.semaphore_signal(barrier, inc=1, device_id=peer(k)[1], device_id_type=MESH)
        return c

    lax.fori_loop(1, n, greet, 0)
    pl.semaphore_wait(barrier, n - 1)

    def half(k):
        to = lax.rem(chip + k, nc)
        return pltpu.make_async_remote_copy(
            src_ref=grads.at[other * nc + to], dst_ref=abuf.at[to], send_sem=asend.at[k], recv_sem=arecv.at[to],
            device_id=partner, device_id_type=MESH)

    def little(k):
        slot, device = peer(k)
        return pltpu.make_async_remote_copy(
            src_ref=small.at[slot], dst_ref=sbuf.at[n - 1 - k], send_sem=ssend.at[k], recv_sem=srecv,
            device_id=device, device_id_type=MESH)

    def spread(k):
        slot, device = peer(k)
        return pltpu.make_async_remote_copy(
            src_ref=own, dst_ref=gsm.at[n - 1 - k], send_sem=gsend.at[k], recv_sem=grecv,
            device_id=device, device_id_type=MESH)

    def piece(k):
        to = lax.rem(chip + k, nc)
        return pltpu.make_async_remote_copy(
            src_ref=comb.at[to], dst_ref=bbuf.at[nc - 1 - k], send_sem=bsend.at[k], recv_sem=brecv,
            device_id=wire.device(core, to), device_id_type=MESH)

    def loop(lo, hi, fn):
        def body(k, c):
            fn(k)
            return c
        lax.fori_loop(lo, hi, body, 0)

    loop(1, n, lambda k: little(k).start())
    loop(0, nc, lambda k: half(lax.rem(k + 1, nc)).start())

    def merge(k):
        to = lax.rem(chip + k, nc)
        half(k).wait_recv()
        comb[pl.ds(to, 1)] = (grads[pl.ds(core * nc + to, 1)].astype(f32) + abuf[pl.ds(to, 1)].astype(f32)).astype(bf)

    def forward(k):
        merge(k)
        piece(k).start()

    loop(1, nc, forward)
    merge(0)

    pltpu.make_async_copy(sbuf, sbuf, srecv).wait()
    total = small[pl.ds(me, 1)][0]
    for k in range(n - 1):
        total = total + sbuf[k]
    own[...] = total
    loop(1, n, lambda k: spread(k).start())

    pltpu.make_async_copy(bbuf, bbuf, brecv).wait()
    total = comb[pl.ds(chip, 1)][0].astype(f32)
    for k in range(nc - 1):
        total = total + bbuf[k].astype(f32)
    res_ref[...] = total

    pltpu.make_async_copy(gsm, gsm, grecv).wait()
    sum_ref[pl.ds(me, 1)] = own[...][None]

    def keep(k):
        sum_ref[pl.ds(lax.rem(me + n - k, n), 1)] = gsm[pl.ds(n - 1 - k, 1)]

    loop(1, n, keep)
    loop(0, nc, lambda k: half(k).wait_send())

    def done(k):
        little(k).wait_send()
        spread(k).wait_send()

    loop(1, n, done)
    loop(1, nc, lambda k: piece(k).wait_send())


def reduce(wire, grads, small):
    n, nc = wire.n, wire.chips
    dma = pltpu.SemaphoreType.DMA
    scratch = [
        pltpu.VMEM((nc, wire.pad, 128), bf),
        pltpu.VMEM((nc, wire.pad, 128), bf),
        pltpu.VMEM((nc - 1, wire.pad, 128), bf),
        pltpu.VMEM((n - 1, 8, 128), f32),
        pltpu.VMEM((8, 128), f32),
        pltpu.VMEM((n - 1, 8, 128), f32),
        dma((nc,)), dma((nc,)), dma((nc,)), dma, dma((n,)), dma, dma((n,)), dma,
    ]
    return staged_call(
        functools.partial(reduce_kernel, wire), (grads, small), [((wire.pad, 128), f32), ((n, 8, 128), f32)], scratch,
        vmem_limit_bytes=60 * 2**20, collective_id=1, has_side_effects=True, name="reduce_gradients")


def finish_kernel(
    wire, res, rows, qkv, proj, fc1, fc2, qkv_bias, proj_bias, fc1_bias, gain1, shift1, gain2, shift2, fc2_bias,
    pool_kernel, pool_gain, pool_bias, rel_h, rel_w,
):
    wide = wire.width
    a, b, c = wire.rows
    qkv[...] = res[0:a, :wide]
    proj[...] = res[a:a + b, :wide]
    fc1[...] = res[a + b:wire.top, :wide]
    fc2[...] = jnp.concatenate(
        [res[wire.top + q * wire.low:wire.top + (q + 1) * wire.low, :wide] for q in range(wire.parts)], 1)
    rel_h[...] = rows[0:REL, :HD]
    rel_w[...] = rows[64:64 + REL, :HD]
    for k in range(9):
        for w in range(2):
            pool_kernel[k, w:w + 1, :] = rows[128 + 9 * w + k:129 + 9 * w + k, :HD]
    pool_gain[...] = rows[146:148, :HD]
    pool_bias[...] = rows[148:150, :HD]
    at = 152
    qkv_bias[...] = jnp.concatenate([rows[at + g:at + g + 1, :HD] for g in range(6)], 1).reshape(3 * D)
    at = 158
    fc1_bias[...] = jnp.concatenate([rows[at + g:at + g + 1, :] for g in range(6)], 1).reshape(FF)
    at = 164
    for k, ref in enumerate((gain1, shift1, gain2, shift2, fc2_bias, proj_bias)):
        first = at + 2 * k
        ref[...] = jnp.concatenate([rows[first:first + 1, :], rows[first + 1:first + 2, :D - 128]], 1).reshape(D)


def finish(wire, res, rows):
    a, b, c = wire.rows
    wide = wire.width
    shapes = [(a, wide), (b, wide), (c, wide), (wire.low, wire.parts * wide), (3 * D,), (D,), (FF,)]
    shapes += [(D,)] * 5 + [(9, 2, HD), (2, HD), (2, HD), (REL, HD), (REL, HD)]
    return staged_call(
        functools.partial(finish_kernel, wire), (res, rows.reshape(-1, 128)), [(v, f32) for v in shapes], [],
        vmem_limit_bytes=60 * 2**20, name="split_gradients")


def compute(wire, block_input, key_crop, cotangent, consts):
    canvases = block_input.shape[0]
    whole = lambda v: pl.BlockSpec(v.shape, lambda i, n=v.ndim: (0,) * n)
    per = lambda: pl.BlockSpec((PAIR, D, NTOK), lambda i: (i, 0, 0))
    packed = [((wire.n, wire.pad, 128), bf), ((wire.n * 8, 128), f32)]
    results = pl.pallas_call(
        functools.partial(kernel, wire),
        grid=(canvases // PAIR,),
        in_specs=[pl.BlockSpec(memory_space=pltpu.SMEM), per(), per()] + [whole(v) for v in consts],
        out_specs=[per(), per()] + [pl.BlockSpec(s, lambda i, n=len(s): (0,) * n) for s, _ in packed],
        out_shape=[jax.ShapeDtypeStruct((canvases, D, NTOK), bf), jax.ShapeDtypeStruct((canvases, D, NTOK), f32)]
        + [jax.ShapeDtypeStruct(*s) for s in packed],
        scratch_shapes=[
            pltpu.VMEM((FEAT, FF), f32), pltpu.VMEM((D, 256), f32), pltpu.VMEM((FEAT, FF), f32),
            pltpu.VMEM((D, FF), f32), pltpu.VMEM((256, 256), f32), pltpu.VMEM((9, 4, 8, 128), f32),
            pltpu.VMEM((2, 4, 8, 128), f32), pltpu.VMEM((5, D, 128), f32), pltpu.VMEM((5, D, 16), f32),
            pltpu.VMEM((4 * D + FF, D), f32), pltpu.VMEM((wire.pad, D), f32),
            pltpu.VMEM((PAIR, 4, KVROWS, 128), f32),
            pltpu.VMEM((PAIR, 4, 272, 128), f32),
            pltpu.VMEM((PAIR, 4, NTOK, 128), f32),
            pltpu.VMEM((PAIR, 2, 256, 256), bf),
            pltpu.VMEM((PAIR, 2, 256, 256), bf),
            pltpu.VMEM((PAIR, 2, 256, 256), bf),
        ],
        compiler_params=pltpu.CompilerParams(vmem_limit_bytes=60 * 2**20),
        name="block_step",
    )(key_crop, jnp.swapaxes(block_input, 1, 2), jnp.swapaxes(cotangent, 1, 2), *consts)
    out, ig, grads, small = results
    return jnp.swapaxes(out, 1, 2), jnp.swapaxes(ig, 1, 2), grads, small


def local(
    wire, block_input, token_crop, key_crop, first_gain, first_bias, qkv_weight, qkv_bias, pool_kernel, pool_gain,
    pool_bias, rel_height, rel_width, proj_weight, proj_bias, second_gain, second_bias, fc1_weight, fc1_bias,
    fc2_weight, fc2_bias, cotangent,
):
    consts = gather(
        wire, (qkv_weight, proj_weight, fc1_weight, fc2_weight),
        (qkv_bias, proj_bias, fc1_bias, first_gain, first_bias, second_gain, second_bias, fc2_bias,
         jnp.transpose(pool_kernel, (1, 0, 2)), pool_gain, pool_bias, rel_height, rel_width))
    out, ig, grads, small = compute(wire, block_input, key_crop, cotangent, consts)
    res, rows = reduce(wire, grads, small.reshape(wire.n, 8, 128))
    (qkv, proj, fc1, fc2, qkv_b, proj_b, fc1_b, gain1, shift1, gain2, shift2, fc2_b, taps, pool_g, pool_s, rel_h,
     rel_w) = finish(wire, res, rows)
    return (out, ig, gain1, shift1, qkv.T, qkv_b, jnp.transpose(taps, (1, 0, 2)), pool_g, pool_s, rel_h, rel_w,
            proj.T, proj_b, gain2, shift2, fc1.T, fc1_b, fc2.T, fc2_b)


def solution(mesh):
    rows = P(("dp", "fsdp"), None, None)
    ids = P(("dp", "fsdp"), None)
    block = P("fsdp", "dp")
    one = P()
    wire = Wire(mesh.shape["dp"], mesh.shape["fsdp"])
    return jax.shard_map(
        functools.partial(local, wire),
        mesh=mesh,
        in_specs=(rows, ids, ids, one, one, block, one, one, one, one, one, one, block, one, one, one, block, one,
                  block, one, rows),
        out_specs=(rows, rows, one, one, block, one, one, one, one, one, one, block, one, one, one, block, one,
                   block, one),
        check_vma=False,
    )
```

```python
import functools

import jax
import jax.numpy as jnp
from jax import lax
from jax.experimental import pallas as pl
from jax.experimental.pallas import tpu as pltpu
from jax.sharding import PartitionSpec as P

D = 192
HEADS = 2
HD = 96
FF = 768
SIDE = 28
KS = 14
NTOK = 784
NKEY = 196
REL = 55

EPS = 1e-06
FILL = -1e30
LOG2E = 1.4426950408889634
LN2 = 0.6931471805599453
SCALE = HD ** (-0.5)
BASE = 32
KVROWS = BASE + NTOK + 24
bf = jnp.bfloat16
PAIR = 2
SKEW = 8
EVERY = 1
FEAT = 208
MAIN = 768
REST = 16
f32 = jnp.float32


def dot(a, b):
    return jnp.dot(a, b, preferred_element_type=f32)


def dot_nt(a, b):
    return lax.dot_general(a, b, (((1,), (1,)), ((), ())), preferred_element_type=f32)


def dot_tn(a, b):
    return lax.dot_general(a, b, (((0,), (0,)), ((), ())), preferred_element_type=f32)


def iota(shape, dim):
    return lax.broadcasted_iota(jnp.int32, shape, dim)


def widen(v):
    return jnp.concatenate([v, jnp.zeros((v.shape[0], 256 - v.shape[1]), v.dtype)], axis=1)


def lanes(col):
    return jnp.concatenate([col] * 6 + [col[:, :16]], axis=1)


def fold_lanes(v):
    total = v[:, 0:128]
    for n in range(1, 6):
        total = total + v[:, 128 * n:128 * n + 128]
    return total


def add_lanes(ref, tail, v):
    ref[...] += fold_lanes(v)
    tail[...] += v[:, 768:784]


def with_ones(v):
    extra = (iota((16, NTOK), 0) < 2).astype(f32).astype(bf)
    return jnp.concatenate([v, extra], 0)


def norm_cols(v):
    mean = jnp.sum(v, 0, keepdims=True) * (1.0 / D)
    c = v - mean
    var = jnp.sum(c * c, 0, keepdims=True) * (1.0 / D)
    r = lax.rsqrt(var + EPS)
    return c * r, r


def norm_cols_back(ge, u, r):
    s1 = jnp.sum(ge, 0, keepdims=True) * (1.0 / D)
    s2 = jnp.sum(ge * u, 0, keepdims=True) * (1.0 / D)
    return (ge - s1 - u * s2) * r


def fold(v):
    total = v[0:8]
    for n in range(1, v.shape[0] // 8):
        total = total + v[8 * n:8 * n + 8]
    return total


def norm_parts(v, mask, width):
    mean = jnp.sum(v, -1, keepdims=True) * (1.0 / width)
    c = (v - mean) * mask
    var = jnp.sum(c * c, -1, keepdims=True) * (1.0 / width)
    r = lax.rsqrt(var + EPS)
    return c * r, r


def norm_back(ge, u, r, width):
    s1 = jnp.sum(ge, -1, keepdims=True) * (1.0 / width)
    s2 = jnp.sum(ge * u, -1, keepdims=True) * (1.0 / width)
    return (ge - s1 - u * s2) * r


def roll_x(tile):
    out = []
    low = iota((8, 128), 0) < 4
    for p in range(KS):
        b = tile[56 * p:56 * p + 56]

        def by(v, n):
            return v if n == 0 else pltpu.roll(v, n, 1)

        out.append(by(b[0:24], 2 * p))
        out.append(jnp.where(low, by(b[24:32], 2 * p), by(b[24:32], 2 * p + 1)))
        out.append(by(b[32:56], 2 * p + 1))
    return out


def roll_y(tile):
    out = []
    low = iota((8, 128), 0) < 4
    for p in range(KS):
        b = tile[56 * p:56 * p + 56]
        out.append(pltpu.roll(b[0:24], 0, 1, stride=1, stride_axis=0))
        mid = b[24:32]
        first = pltpu.roll(mid, 24, 1, stride=1, stride_axis=0)
        second = pltpu.roll(pltpu.roll(mid, 124, 1), 0, 1, stride=1, stride_axis=0)
        out.append(jnp.where(low, first, second))
        out.append(pltpu.roll(b[32:56], 4, 1, stride=1, stride_axis=0))
    return out


def kernel(
    wire, steps_of, kc_ref, x_ref, g_ref, wq_ref, wpt_ref, w1_ref, w2t_ref, wqt_ref, wp_ref, w1t_ref, w2_ref,
    relf_ref, relb_ref, vec_ref, pk_ref, pv_ref,
    out_ref, ig_ref, wire_ref, small_ref,
    gq_ref, gp_ref, g1_ref, g2_ref, grel_ref, gpk_ref, gpv_ref, gln_ref, tail_ref, table, piece,
    kvs, gps, gkvs, kf, kb, vx, *spare,
):
    step = pl.program_id(0)
    spare = [(spare[2 * k], spare[2 * k + 1]) for k in range(4)]

    @pl.when(step == 0)
    def _():
        for ref in (gq_ref, gp_ref, g1_ref, g2_ref, grel_ref, gpk_ref, gpv_ref, gln_ref, tail_ref):
            ref[...] = jnp.zeros_like(ref)
        kvs[...] = jnp.zeros_like(kvs)
        gps[...] = jnp.zeros_like(gps)
        key = iota((256, 128), 0)
        lane = iota((256, 128), 1)
        ki = key >> 4
        kj = key & 15
        spot = lane & 63
        low = lane < 64
        real = (kj < KS) & (ki < KS)
        for c, h in [(c, h) for c in range(PAIR) for h in range(HEADS)]:
            first, second = (ki, kj) if h == 0 else (kj, ki)
            which = jnp.where(low, first, second)
            kf[c, h, :, 128:] = jnp.where((spot == 27 + 2 * which) & real, 1.0, 0.0).astype(bf)
            kb[c, h, :, 128:] = jnp.where((spot == 26 - 2 * which) & real, 1.0, 0.0).astype(bf)
            kf[c, h, :, :128] = jnp.where((lane == HD) & (key >= 0), FILL, 0.0).astype(bf)
            kb[c, h, :, :128] = jnp.zeros((256, 128), bf)
            vx[c, h, :, :128] = jnp.zeros((256, 128), bf)
            vx[c, h, :, 128:] = jnp.ones((256, 128), bf)

    pairs = Pairs(step, dict(gq=gq_ref, gp=gp_ref, g1=g1_ref, g2=g2_ref), dict(zip(("gq", "gp", "g1", "g2"), spare)))
    later = pairs.later
    steps = [
        canvas(
            pairs, step * PAIR + c, c, kc_ref, x_ref, g_ref, wq_ref, wpt_ref, w1_ref, w2t_ref, wqt_ref, wp_ref, w1t_ref, w2_ref,
            relf_ref, relb_ref, vec_ref, pk_ref, pv_ref,
            out_ref, ig_ref, gq_ref, gp_ref, g1_ref, g2_ref, grel_ref, gpk_ref, gpv_ref, gln_ref, tail_ref,
            kvs.at[c], gps.at[c], gkvs.at[c], kf.at[c], kb.at[c], vx.at[c])
        for c in range(PAIR)]
    live = list(steps)
    tick = 0
    while live:
        for c, one in enumerate(steps):
            if one in live and tick >= c * SKEW:
                try:
                    next(one)
                except StopIteration:
                    live.remove(one)
                if later and tick % EVERY == 0:
                    later.pop(0)()
        tick += 1
    while later:
        later.pop(0)()

    @pl.when(step == pl.num_programs(0) - 1)
    def _():
        pairs.finish(steps_of)
        pack(wire, wq_ref, w1_ref, vec_ref, wire_ref, small_ref, gq_ref, gp_ref, g1_ref, g2_ref, grel_ref, gpk_ref, gpv_ref, gln_ref,
             tail_ref, table, piece)


def pack(wire, wq_ref, w1_ref, vec_ref, wire_ref, small_ref, gq_ref, gp_ref, g1_ref, g2_ref, grel_ref, gpk_ref, gpv_ref, gln_ref, tail_ref,
         table, piece):
    wide = wire.width
    gain1, shift1, gain2, shift2 = [vec_ref[k] for k in range(4)]
    norm_rows = []
    for ref, w_ref, gain, shift in ((gq_ref, wq_ref, gain1, shift1), (g1_ref, w1_ref, gain2, shift2)):
        by_gain, by_shift = 0.0, 0.0
        for g in range(6):
            cols = slice(128 * g, 128 * g + 128)
            w = w_ref[:D, cols].astype(f32)
            sums = ref[D:D + 1, cols]
            by_gain = by_gain + w * ref[:D, cols]
            by_shift = by_shift + w * sums
            ref[:D, cols] = gain * ref[:D, cols] + shift * sums
        for v in (by_gain, by_shift):
            norm_rows.append(jnp.sum(jnp.transpose(v / gain), 0, keepdims=True))
    for g in range(6):
        table[HD * g:HD * g + HD, :] = jnp.transpose(gq_ref[:D, 128 * g:128 * g + 128])[:HD]
    table[3 * D:4 * D, :] = jnp.concatenate([gp_ref[:, 0:HD], gp_ref[:, 128:128 + HD]], 1)
    table[4 * D:4 * D + FF, :] = jnp.transpose(g1_ref[:D])
    piece[...] = jnp.zeros_like(piece)
    for d in range(wire.dp):
        for first, count, at in wire.starts(d):
            piece[first:first + count, :] = table[at:at + count, :]
        low = g2_ref[wire.low * d:wire.low * (d + 1), :] * 0.5
        for f in range(wire.fsdp):
            for q in range(wire.parts):
                first = wire.top + q * wire.low
                at = (f * wire.parts + q) * wide
                piece[first:first + wire.low, f * wide:(f + 1) * wide] = low[:, at:at + wide]
        for f in range(wire.fsdp):
            part = piece[:, f * wide:(f + 1) * wide]
            wire_ref[wire.slot(d, f)] = wire.fold(part[:wire.top], part[wire.top:wire.used]).astype(bf)
    small_ref[...] = jnp.zeros_like(small_ref)
    turned = jnp.transpose(grel_ref[...]) * LOG2E
    small_ref[0:64] = turned[0:64, 0:128] + turned[64:128, 128:256]
    small_ref[64:128] = turned[192:256, 0:128] + turned[128:192, 128:256]
    for w in range(2):
        for k in range(9):
            small_ref[128 + 9 * w + k:129 + 9 * w + k] = jnp.sum(
                gpk_ref[k, 2 * w] + gpk_ref[k, 2 * w + 1], 0, keepdims=True)
        for m in range(2):
            small_ref[146 + 2 * m + w:147 + 2 * m + w] = jnp.sum(
                gpv_ref[m, 2 * w] + gpv_ref[m, 2 * w + 1], 0, keepdims=True)
    for g in range(6):
        small_ref[152 + g:153 + g] = gq_ref[D:D + 1, 128 * g:128 * g + 128]
        small_ref[158 + g:159 + g] = g1_ref[D:D + 1, 128 * g:128 * g + 128]
    rows = norm_rows + [jnp.sum(jnp.transpose(gln_ref[...]), 0, keepdims=True)
                        + jnp.sum(jnp.transpose(tail_ref[...]), 0, keepdims=True)]
    rows.append(jnp.transpose(gp_ref[:, 0:128])[HD:HD + 1])
    for k, v in enumerate(rows):
        small_ref[164 + 2 * k:165 + 2 * k] = v[:, 0:128]
        small_ref[165 + 2 * k:166 + 2 * k] = jnp.concatenate([v[:, 128:D], jnp.zeros((1, 256 - D), f32)], 1)


def features(v, w):
    return jnp.transpose(dot(v, w)[:, :D])


def add_dot(ref, cols, left, right):
    ref[:, cols] += dot(left, right)


class Pairs:
    def __init__(self, step, totals, spare):
        self.step, self.totals, self.spare = step, totals, spare
        self.later, self.held = [], {}

    def add(self, name, slot, left, right):
        self.held.setdefault(name, []).append((slot, left, right))
        if len(self.held[name]) < PAIR:
            return
        both = sorted(self.held.pop(name), key=lambda v: v[0])
        total = self.totals[name]
        left = jnp.concatenate([v[1][:, :MAIN] for v in both], 1)
        right = jnp.concatenate([v[2][:MAIN] for v in both], 0)
        for n in range(0, right.shape[1], 256):
            cols = slice(n, n + 256)
            self.later.append(functools.partial(add_dot, total, cols, left, right[:, cols]))
        keep_left, keep_right = self.spare[name]
        keep_left[self.step] = jnp.concatenate([v[1][:, MAIN:] for v in both], 1)
        rows = PAIR * REST
        keep_right[pl.ds(pl.multiple_of(self.step * rows, rows), rows), :] = jnp.concatenate([v[2][MAIN:] for v in both], 0)

    def finish(self, steps):
        for name, total in self.totals.items():
            keep_left, keep_right = self.spare[name]
            left = jnp.concatenate([keep_left[k] for k in range(steps)], 1)
            total[...] += dot(left, keep_right[...])


def canvas(
    pairs, item, slot, kc_ref, x_ref, g_ref, wq_ref, wpt_ref, w1_ref, w2t_ref, wqt_ref, wp_ref, w1t_ref, w2_ref,
    relf_ref, relb_ref, vec_ref, pk_ref, pv_ref,
    out_ref, ig_ref, gq_ref, gp_ref, g1_ref, g2_ref, grel_ref, gpk_ref, gpv_ref, gln_ref, tail_ref,
    kvs, gps, gkvs, kf, kb, vx,
):
    lane128 = iota((1, 128), 1)
    mask96 = (lane128 < HD).astype(f32)
    lowhalf = iota((NTOK, 128), 1) < 64

    fc2_bias = lanes(vec_ref[4])

    x = x_ref[slot].astype(f32)
    u1, r1 = norm_cols(x)
    nb = with_ones(u1.astype(bf))
    qb = dot_tn(nb, wq_ref[:, :256]).astype(bf)
    for n in range(4):
        kvs[n, BASE:BASE + NTOK, :] = dot_tn(nb, wq_ref[:, 256 + 128 * n:384 + 128 * n])

    yield
    notfirst = (iota((16, 128), 0) > 0).astype(f32)

    def tap(n, x_row, b):
        v = kvs.at[n][pl.ds(BASE + SIDE * x_row + b - 1, 16, stride=2), :]
        return v

    u_pool, r_pool = [], []
    for n in range(4):
        w = n // 2
        taps = [pk_ref[w, k:k + 1] for k in range(9)]
        taps = [v * notfirst if k % 3 == 0 else v for k, v in enumerate(taps)]
        rows = []
        for i in range(KS):
            acc = None
            for a in range(3):
                for b in range(3):
                    t = tap(n, 2 * i + a - 1, b) * taps[3 * a + b]
                    acc = t if acc is None else acc + t
            rows.append(acc)
        u, r = norm_parts(jnp.concatenate(rows, 0), mask96, HD)
        u_pool.append(u)
        r_pool.append(r)
        val = u * pv_ref[w:w + 1] + pv_ref[2 + w:3 + w]
        yield
        h = n % 2
        if w == 0:
            val = val * (SCALE * LOG2E)
            kb[h, 0:224, :128] = val.astype(bf)
            pad = ((iota((224, 128), 0) & 15) >= KS) & (iota((224, 128), 1) == HD)
            kf[h, 0:224, :128] = jnp.where(pad, FILL, val).astype(bf)
        else:
            vx[h, 0:224, :128] = val.astype(bf)

    row_cut = 0
    col_cut = 0
    for n in range(KS):
        row_cut = row_cut + jnp.where(kc_ref[item, KS * n] < 2, 2, 0)
        col_cut = col_cut + jnp.where((kc_ref[item, n] & 1) == 0, 2, 0)
    spot = (lane128 & 63) - 27
    row_side = spot >= row_cut
    col_side = spot >= col_cut
    rows_before = jnp.where(row_side, FILL, 0.0)
    rows_after = jnp.where(row_side, 0.0, FILL)
    y56 = iota((56, 128), 0)
    y56 = jnp.where(y56 >= SIDE, y56 - SIDE, y56)
    col_bias = jnp.where((y56 >= col_cut) != col_side, FILL, 0.0)

    yield
    a_h = dot(qb, relf_ref[:, :128])
    a_w = dot(qb, relf_ref[:, 128:])
    pieces_h = roll_x(a_h)
    yield
    pieces_w = roll_y(a_w)
    done_h, done_w = [], []
    for p in range(KS):
        row_bias = jnp.where(2 * p >= row_cut, rows_after, rows_before)
        done_h.append(jnp.concatenate(pieces_h[3 * p:3 * p + 3], 0) + row_bias)
        done_w.append(jnp.concatenate(pieces_w[3 * p:3 * p + 3], 0) + col_bias)
    yield
    t_h = jnp.concatenate(done_h, 0)
    t_w = jnp.concatenate(done_w, 0)
    rel = (jnp.where(lowhalf, t_h, t_w).astype(bf), jnp.where(lowhalf, t_w, t_h).astype(bf))

    yield
    eb, inv, mixed = [], [], []
    for h in range(HEADS):
        left = jnp.concatenate([qb[:, 128 * h:128 * h + 128], rel[h]], 1)
        s = dot_nt(left, kf[h])
        e = jnp.exp2(s - jnp.max(s, -1, keepdims=True)).astype(bf)
        yield
        o = dot(e, vx[h])
        rinv = 1.0 / o[:, 128:]
        eb.append(e)
        inv.append(rinv * LN2)
        mixed.append(o[:, :128] * rinv)
    yield
    ab = (jnp.concatenate(mixed, 1) + qb.astype(f32)).astype(bf)

    yield
    middle = x + features(ab, wp_ref[...])
    u2, r2 = norm_cols(middle)
    n2b = with_ones(u2.astype(bf))
    gb = g_ref[slot]
    yield
    act, gh = [], []
    for n in range(3):
        cols = slice(256 * n, 256 * n + 256)
        hid = dot_tn(n2b, w1_ref[:, cols])
        gact = dot_tn(gb, w2t_ref[:, cols])
        yield
        z = hid * 0.7071067811865476
        phi = 1.0 + lax.erf(z)
        slope = phi + z * (jnp.exp2(z * z * (-LOG2E)) * 1.1283791670955126)
        act.append((hid * phi).astype(bf))
        gh.append((gact * slope).astype(bf))
        yield
    act = jnp.concatenate(act, 1)
    gh = jnp.concatenate(gh, 1)
    out = middle + fc2_bias + features(act, w2_ref[...])
    out_ref[slot] = out.astype(bf)
    pairs.add("g2", slot, gb, act)
    pairs.add("g1", slot, n2b, gh)
    yield
    g = gb.astype(f32)
    add_lanes(gln_ref, tail_ref, g)
    ge = features(gh, w1t_ref[...])
    yield
    gm = g + norm_cols_back(ge, u2, r2)
    grb = gm.astype(bf)
    pairs.add("gp", slot, grb, ab)
    yield
    yield
    gatt = dot_tn(grb, wpt_ref[...])
    gr, gcont = [], []
    g2bs, dss = [], []
    for h in range(HEADS):
        ga = gatt[:, 128 * h:128 * h + 128]
        ga = ga * inv[h]
        g2b = ga.astype(bf)
        dd = jnp.sum(ga * mixed[h], -1, keepdims=True)
        yield
        gpr = dot_nt(g2b, vx[h, :, :128])
        ds = eb[h] * (gpr - dd).astype(bf)
        yield
        back = dot(ds, kb[h])
        gcont.append(back[:, :128])
        gr.append(back[:, 128:])
        dss.append(ds)
        g2bs.append(g2b)
    yield
    b_h = jnp.concatenate(roll_x(jnp.where(lowhalf, gr[0], gr[1])), 0)
    yield
    b_w = jnp.concatenate(roll_y(jnp.where(lowhalf, gr[1], gr[0])), 0)
    gab = jnp.concatenate([b_h, b_w], 1).astype(bf)
    gq = jnp.concatenate(gcont, 1) + dot(gab, relb_ref[...]) + gatt

    yield
    for n in range(4):
        w, h = n // 2, n % 2
        if w == 0:
            qt = dot_tn(qb[:, 128 * h:128 * h + 128], jnp.concatenate([dss[h], gab], 1))
            grel_ref[128 * h:128 * h + 128] += qt[:, 256:]
            e = jnp.transpose(qt[:, :256])[:224] * (SCALE * LOG2E)
        else:
            e = jnp.transpose(dot_tn(g2bs[h], eb[h]))[:224] * LOG2E
        yield
        gpv_ref[0, n] += fold(e * u_pool[n])
        gpv_ref[1, n] += fold(e)
        gps[n, 0:224, :] = norm_back(e * pv_ref[w:w + 1], u_pool[n], r_pool[n], HD)

    for n in range(4):
        w = n // 2
        for a in range(3):
            yield
            for b in range(3):
                acc = None
                for i in range(KS):
                    t = gps[n, 16 * i:16 * i + 16, :] * tap(n, 2 * i + a - 1, b)
                    acc = t if acc is None else acc + t
                if b == 0:
                    acc = acc * notfirst
                gpk_ref[3 * a + b, n] += acc[0:8] + acc[8:16]


        yield
        def wk(a, b):
            return pk_ref[w, 3 * a + b:3 * a + b + 1]

        for i in range(KS):
            p0 = gps[n, 16 * i:16 * i + 16, :]
            p0s = gps[n, 16 * i + 1:16 * i + 17, :]
            p1 = gps[n, 16 * i + 16:16 * i + 32, :]
            p1s = gps[n, 16 * i + 17:16 * i + 33, :]
            even = SIDE * 2 * i
            odd = even + SIDE
            ee = p0 * wk(1, 1)
            eo = p0 * wk(1, 2) + p0s * wk(1, 0)
            oe = p0 * wk(2, 1) + p1 * wk(0, 1)
            oo = p0 * wk(2, 2) + p0s * wk(2, 0) + p1 * wk(0, 2) + p1s * wk(0, 0)
            gk = gkvs.at[n]
            gk[pl.ds(even, KS, stride=2), :] = ee[:KS]
            gk[pl.ds(even + 1, KS, stride=2), :] = eo[:KS]
            gk[pl.ds(odd, KS, stride=2), :] = oe[:KS]
            gk[pl.ds(odd + 1, KS, stride=2), :] = oo[:KS]

    yield
    gpk = jnp.concatenate([gq.astype(bf)] + [gkvs[n].astype(bf) for n in range(4)], 1)
    pairs.add("gq", slot, nb, gpk)
    ge = features(gpk, wqt_ref[...])
    yield
    ig_ref[slot] = gm + norm_cols_back(ge, u1, r1)


MESH = pl.DeviceIdType.MESH


class Wire:
    def __init__(self, dp, fsdp):
        self.dp, self.fsdp, self.n = dp, fsdp, dp * fsdp
        self.chips = self.n // 2
        self.line, self.plane = dp // 4, 2 * fsdp
        self.rows = (3 * D // dp, D // dp, FF // dp)
        self.top = sum(self.rows)
        self.low = D // dp
        self.width = D // fsdp
        self.parts = FF // fsdp // self.width
        self.used = self.top + self.parts * self.low
        self.pad = -(-self.used // 16) * 16
        self.lows = self.parts * self.low
        self.dense = self.width == 96 and self.top == 2 * self.lows and self.lows % 48 == 0
        self.full = self.top + self.lows // 3 if self.dense else self.pad

    def fold(self, top, low, *more):
        rows = self.lows
        if self.dense:
            third = rows // 3
            parts = [
                jnp.concatenate([top[:rows], low[:, 0:32]], 1),
                jnp.concatenate([top[rows:], low[:, 32:64]], 1),
                jnp.concatenate([low[k * third:(k + 1) * third, 64:96] for k in range(3)]
                                + [jnp.zeros((third, 32), top.dtype)], 1)]
        else:
            parts = [jnp.concatenate([v, jnp.zeros((v.shape[0], 128 - self.width), top.dtype)], 1) for v in (top, low)]
            if self.pad > self.used:
                parts.append(jnp.zeros((self.pad - self.used, 128), top.dtype))
        return jnp.concatenate(parts + list(more), 0)

    def unfold(self, block):
        rows, wide = self.lows, self.width
        if not self.dense:
            return block[:self.top, :wide], block[self.top:self.used, :wide]
        third = rows // 3
        last = jnp.concatenate([block[self.top:self.top + third, 32 * k:32 * k + 32] for k in range(3)], 0)
        low = jnp.concatenate([block[:rows, 96:128], block[rows:2 * rows, 96:128], last], 1)
        return block[:self.top, :wide], low

    def starts(self, d):
        a, b, c = self.rows
        return ((0, a, a * d), (a, b, 3 * D + b * d), (a + b, c, 4 * D + c * d))

    def slot(self, d, f):
        return (d % 2) * self.chips + ((d // 2) % 2 * self.fsdp + f) * self.line + d // 4

    def place(self):
        d, f = lax.axis_index("dp"), lax.axis_index("fsdp")
        return lax.rem(d, 2), lax.rem(d // 2, 2) * self.fsdp + f, d // 4

    def peer(self, slot):
        chip = lax.rem(slot, self.chips)
        return self.device(slot // self.chips, chip // self.line, lax.rem(chip, self.line))

    def device(self, core, q, z):
        return (4 * z + 2 * (q // self.fsdp) + core, lax.rem(q, self.fsdp))


def greet_near(wire):
    line, plane = wire.line, wire.plane
    core, q, z = wire.place()
    friends = [wire.device(1 - core, q, z)]
    friends += [wire.device(core, q, lax.rem(z + k, line)) for k in range(1, line)]
    friends += [wire.device(core, lax.rem(q + j, plane), z) for j in range(1, plane)]
    for friend in friends:
        pl.semaphore_signal(pltpu.get_barrier_semaphore(), inc=1, device_id=friend, device_id_type=MESH)


def gather_kernel(
    wire, qkv, proj, fc1, fc2, qkv_bias, proj_bias, fc1_bias, gain1, shift1, gain2, shift2, fc2_bias,
    pool_kernel, pool_gain, pool_bias, rel_h, rel_w,
    wq_ref, wpt_ref, w1_ref, w2t_ref, wqt_ref, wp_ref, w1t_ref, w2_ref, relf_ref, relb_ref, vec_ref, pk_ref, pv_ref,
    buf, tmp, table, low_table, line_send, plane_send, core_send, recv,
):
    nc, line, plane = wire.chips, wire.line, wire.plane
    core, q, z = wire.place()
    other = 1 - core
    me = core * nc + q * line + z
    wide = wire.width
    a, b, c = wire.rows
    tmp[...] = jnp.zeros_like(tmp)
    tmp[0:a, :wide] = qkv[...].astype(f32)
    tmp[a:a + b, :wide] = proj[...].astype(f32)
    tmp[a + b:wire.top, :wide] = fc1[...].astype(f32)
    below = fc2[...].astype(f32)
    for p in range(wire.parts):
        first = wire.top + p * wire.low
        tmp[first:first + wire.low, :wide] = below[:, p * wide:(p + 1) * wide]
    buf[pl.ds(me, 1)] = tmp[:, :128].astype(bf)[None]
    pl.semaphore_wait(pltpu.get_barrier_semaphore(), line + plane - 1)

    def held(k, j):
        return core * nc + lax.rem(q + j, plane) * line + lax.rem(z + k, line)

    def copy(slot, sem, device):
        return pltpu.make_async_remote_copy(
            src_ref=buf.at[slot], dst_ref=buf.at[slot], send_sem=sem, recv_sem=recv.at[slot],
            device_id=device, device_id_type=MESH)

    def to_line(k):
        return copy(me, line_send.at[k], wire.device(core, q, lax.rem(z + k, line)))

    def to_plane(k, j):
        return copy(held(k, 0), plane_send.at[k * plane + j], wire.device(core, lax.rem(q + j, plane), z))

    def to_core(k, j):
        return copy(held(k, j), core_send.at[k * plane + j], wire.device(other, q, z))

    for k in range(1, line):
        to_line(k).start()
    for j in range(1, plane):
        to_plane(0, j).start()
    to_core(0, 0).start()

    def row(ref):
        return ref[...].reshape(1, ref.shape[0])

    for k, ref in enumerate((gain1, shift1, gain2, shift2, fc2_bias)):
        vec_ref[k] = jnp.transpose(jnp.broadcast_to(row(ref), (128, D)))
    zero32 = jnp.zeros((64, 128 - HD), f32)

    def tall(ref):
        t = jnp.concatenate([ref[...] * LOG2E, jnp.zeros((64 - REL, HD), f32)], 0)
        t = jnp.concatenate([t, zero32], 1)
        return jnp.where(iota((64, 128), 0) < 54, t, 0.0)

    th, tw = tall(rel_h), tall(rel_w)
    none = jnp.zeros((64, 128), f32)
    relb = jnp.concatenate([
        jnp.concatenate([th, none], 1), jnp.concatenate([none, th], 1),
        jnp.concatenate([none, tw], 1), jnp.concatenate([tw, none], 1)], 0).astype(bf)
    relb_ref[...] = relb
    at, to = iota((256, 256), 0), iota((256, 256), 1)
    mirror = ((at >> 6) == (to >> 6)) & ((at & 63) + (to & 63) == 53)
    relf_ref[...] = dot_tn(relb, jnp.where(mirror, 1.0, 0.0).astype(bf)).astype(bf)
    for w in range(2):
        taps = jnp.concatenate([pool_kernel[k, w:w + 1, :] for k in range(9)], 0)
        pk_ref[w] = jnp.concatenate([taps, jnp.zeros((9, 128 - HD), f32)], 1)
    four = jnp.concatenate([pool_gain[...], pool_bias[...]], 0)
    pv_ref[...] = jnp.concatenate([four, jnp.zeros((4, 128 - HD), f32)], 1)

    for k in range(1, line):
        to_core(k, 0).wait_recv()
        for j in range(1, plane):
            to_plane(k, j).start()
        to_core(k, 0).start()
    for k in range(line):
        for j in range(1, plane):
            to_core(k, j).wait_recv()
            to_core(k, j).start()
    for c in range(nc):
        copy(other * nc + c, core_send.at[0], wire.device(other, q, z)).wait_recv()

    for d in range(wire.dp):
        blocks = [buf[wire.slot(d, f)].astype(f32) for f in range(wire.fsdp)]
        tmp[...] = jnp.concatenate([v[:, :wide] for v in blocks], 1)
        for first, count, to_row in wire.starts(d):
            table[to_row:to_row + count, :] = tmp[first:first + count, :]
        for f in range(wire.fsdp):
            parts = [tmp[wire.top + q * wire.low:wire.top + (q + 1) * wire.low, f * wide:(f + 1) * wide]
                     for q in range(wire.parts)]
            low_table[wire.low * d:wire.low * (d + 1), f * wide * wire.parts:(f + 1) * wide * wire.parts] = (
                jnp.concatenate(parts, 1))

    def two(bias):
        hi = bias.astype(bf).astype(f32)
        return jnp.concatenate([hi, bias - hi, jnp.zeros((14, bias.shape[1]), f32)], 0)

    qb = row(qkv_bias)
    for g in range(6):
        w = jnp.transpose(table[HD * g:HD * g + HD, :])
        bias = qb[:, HD * g:HD * g + HD] + jnp.sum(w * vec_ref[1][:, :HD], 0, keepdims=True)
        block = jnp.concatenate([w * vec_ref[0][:, :HD], two(bias)], 0)
        spare = (iota((FEAT, 128 - HD), 0) == D) & (iota((FEAT, 128 - HD), 1) == 0) & (g < 2)
        block = jnp.concatenate([block, jnp.where(spare, 1.0, 0.0)], 1)
        wq_ref[:, 128 * g:128 * g + 128] = block.astype(bf)
        flat = table[HD * g:HD * g + HD, :] * row(gain1)
        flat = jnp.concatenate([flat, jnp.zeros((128 - HD, D), f32)], 0)
        wqt_ref[128 * g:128 * g + 128, :] = widen(flat).astype(bf)
    cols = []
    pb = row(proj_bias)
    hi = pb.astype(bf).astype(f32)
    for g, extra in enumerate((hi, pb - hi)):
        col = jnp.transpose(jnp.broadcast_to(extra, (128, D)))[:, :128 - HD]
        col = jnp.where(iota((D, 128 - HD), 1) == 0, col, 0.0)
        cols += [table[3 * D:4 * D, HD * g:HD * g + HD], col]
    wpt = jnp.concatenate(cols, 1)
    wpt_ref[...] = wpt.astype(bf)
    wp_ref[...] = widen(jnp.transpose(wpt)).astype(bf)
    w1t_ref[...] = widen(table[4 * D:4 * D + FF, :] * row(gain2)).astype(bf)
    w2_ref[...] = widen(jnp.transpose(low_table[...]) * 0.5).astype(bf)
    fb = row(fc1_bias)
    for g in range(6):
        w = jnp.transpose(table[4 * D + 128 * g:4 * D + 128 * g + 128, :])
        bias = fb[:, 128 * g:128 * g + 128] + jnp.sum(w * vec_ref[3], 0, keepdims=True)
        w1_ref[:, 128 * g:128 * g + 128] = jnp.concatenate([w * vec_ref[2], two(bias)], 0).astype(bf)
    w2t_ref[...] = (low_table[...] * 0.5).astype(bf)

    for k in range(line):
        if k:
            to_line(k).wait_send()
        for j in range(plane):
            if j:
                to_plane(k, j).wait_send()
            to_core(k, j).wait_send()


def staged(body, hello, ins, outs, *refs):
    a, b = len(ins), len(outs)
    src, dst = refs[:a], refs[a:a + b]
    vin, vout = refs[a + b:2 * a + b], refs[2 * a + b:2 * (a + b)]
    sems, rest = refs[2 * (a + b)], refs[2 * (a + b) + 1:]
    hello()
    loads = [pltpu.make_async_copy(s, v, sems.at[k]) for k, (s, v) in enumerate(zip(src, vin))]
    for c in loads:
        c.start()
    for c in loads:
        c.wait()
    body(*vin, *vout, *rest)
    stores = [pltpu.make_async_copy(v, d, sems.at[k]) for k, (v, d) in enumerate(zip(vout, dst))]
    for c in stores:
        c.start()
    for c in stores:
        c.wait()


def staged_call(body, args, shapes, scratch, hello=lambda: None, **params):
    hbm = pl.BlockSpec(memory_space=pltpu.HBM)
    ins = [(v.shape, v.dtype) for v in args]
    name = params.pop("name")
    return pl.pallas_call(
        functools.partial(staged, body, hello, ins, shapes),
        in_specs=[hbm] * len(ins),
        out_specs=[hbm] * len(shapes),
        out_shape=[jax.ShapeDtypeStruct(*s) for s in shapes],
        scratch_shapes=[pltpu.VMEM(*s) for s in ins + list(shapes)]
        + [pltpu.SemaphoreType.DMA((max(len(ins), len(shapes)),))] + list(scratch),
        compiler_params=pltpu.CompilerParams(**params),
        name=name,
    )(*args)


def gather(wire, shards, vectors):
    shapes = [((FEAT, FF), bf), ((D, 256), bf), ((FEAT, FF), bf), ((D, FF), bf), ((FF, 256), bf), ((256, 256), bf), ((FF, 256), bf), ((FF, 256), bf),
              ((256, 256), bf), ((256, 256), bf),
              ((5, D, 128), f32), ((2, 9, 128), f32), ((4, 128), f32)]
    args = [v.T for v in shards] + list(vectors)
    scratch = [
        pltpu.VMEM((wire.n, wire.pad, 128), bf),
        pltpu.VMEM((wire.pad, D), f32),
        pltpu.VMEM((4 * D + FF, D), f32),
        pltpu.VMEM((D, FF), f32),
        pltpu.SemaphoreType.DMA((wire.line,)),
        pltpu.SemaphoreType.DMA((wire.chips,)),
        pltpu.SemaphoreType.DMA((wire.chips,)),
        pltpu.SemaphoreType.DMA((wire.n,)),
    ]
    return staged_call(
        functools.partial(gather_kernel, wire), args, shapes, scratch, functools.partial(greet_near, wire),
        vmem_limit_bytes=60 * 2**20, collective_id=0, has_side_effects=True, name="gather_weights")


def greet_all(wire):
    core, q, z = wire.place()
    me = core * wire.chips + q * wire.line + z

    def one(k, c):
        pl.semaphore_signal(pltpu.get_barrier_semaphore(), inc=1, device_id=wire.peer(lax.rem(me + k, wire.n)),
                            device_id_type=MESH)
        return c

    lax.fori_loop(1, wire.n, one, 0)


def reduce_kernel(
    wire, grads, small, res_ref, sum_ref,
    abuf, sa, comb, scomb, bbuf, sb, comb2, scomb2, cbuf, sc, own, gsm,
    asend, arecv, sasend, sarecv, bsend, brecv, sbsend, sbrecv, csend, crecv, scsend, screcv, gsend, grecv,
):
    n, nc, line, plane = wire.n, wire.chips, wire.line, wire.plane
    core, q, z = wire.place()
    other = 1 - core
    me = core * nc + q * line + z

    def peer(k):
        return wire.peer(lax.rem(me + k, n))

    def loop(lo, hi, fn):
        def body(k, c):
            fn(k)
            return c
        lax.fori_loop(lo, hi, body, 0)

    pl.semaphore_wait(pltpu.get_barrier_semaphore(), n - 1)

    def remote(src, dst, send, recv, device):
        return pltpu.make_async_remote_copy(
            src_ref=src, dst_ref=dst, send_sem=send, recv_sem=recv, device_id=device, device_id_type=MESH)

    def plane_at(j):
        return lax.rem(q + j, plane)

    def line_at(k):
        return lax.rem(z + k, line)

    partner = wire.device(other, q, z)
    small_a = remote(small.at[pl.ds(other * nc, nc)], sa, sasend, sarecv, partner)

    def half(j):
        at = plane_at(j) * line
        return remote(grads.at[pl.ds(other * nc + at, line)], abuf.at[pl.ds(at, line)], asend.at[j], arecv.at[j], partner)

    def group(j):
        return remote(comb.at[pl.ds(plane_at(j) * line, line)], bbuf.at[j - 1], bsend.at[j], brecv.at[j],
                      wire.device(core, plane_at(j), z))

    def small_b(j):
        return remote(scomb.at[pl.ds(plane_at(j) * line, line)], sb.at[j - 1], sbsend.at[j], sbrecv.at[j],
                      wire.device(core, plane_at(j), z))

    def last(k):
        return remote(comb2.at[line_at(k)], cbuf.at[k - 1], csend.at[k], crecv.at[k], wire.device(core, q, line_at(k)))

    def small_c(k):
        return remote(scomb2.at[line_at(k)], sc.at[k - 1], scsend.at[k], screcv.at[k],
                      wire.device(core, q, line_at(k)))

    def spread(k):
        return remote(own, gsm.at[n - 1 - k], gsend.at[k], grecv, peer(k))

    order = list(range(1, plane)) + [0]
    small_a.start()
    for j in order:
        half(j).start()
    small_a.wait_recv()
    scomb[...] = small[pl.ds(core * nc, nc)] + sa[...]
    for j in range(1, plane):
        small_b(j).start()
    for j in order:
        half(j).wait_recv()
        at = pl.ds(plane_at(j) * line, line)
        both = grads[pl.ds(core * nc + plane_at(j) * line, line)].astype(f32) + abuf[at].astype(f32)
        comb[at] = both.astype(bf)
        if j:
            group(j).start()
    mine = pl.ds(q * line, line)
    total = scomb[mine]
    for j in range(1, plane):
        small_b(j).wait_recv()
        total = total + sb[j - 1]
    scomb2[...] = total
    for k in range(1, line):
        small_c(k).start()
    total = scomb2[pl.ds(z, 1)][0]
    for k in range(1, line):
        small_c(k).wait_recv()
        total = total + sc[k - 1]
    own[...] = total
    loop(1, n, lambda k: spread(k).start())
    total = comb[mine].astype(f32)
    for j in range(1, plane):
        group(j).wait_recv()
        total = total + bbuf[j - 1].astype(f32)
    comb2[...] = total.astype(bf)
    for k in range(1, line):
        last(k).start()
    total = comb2[pl.ds(z, 1)][0].astype(f32)
    for k in range(1, line):
        last(k).wait_recv()
        total = total + cbuf[k - 1].astype(f32)
    res_ref[...] = total
    pltpu.make_async_copy(gsm, gsm, grecv).wait()
    sum_ref[pl.ds(me, 1)] = own[...][None]

    def keep(k):
        sum_ref[pl.ds(lax.rem(me + n - k, n), 1)] = gsm[pl.ds(n - 1 - k, 1)]

    loop(1, n, keep)
    small_a.wait_send()
    for j in range(plane):
        half(j).wait_send()
        if j:
            group(j).wait_send()
            small_b(j).wait_send()
    for k in range(1, line):
        last(k).wait_send()
        small_c(k).wait_send()
    loop(1, n, lambda k: spread(k).wait_send())


def reduce(wire, grads, small):
    n, nc, line, plane = wire.n, wire.chips, wire.line, wire.plane
    dma = pltpu.SemaphoreType.DMA
    big = lambda *lead: pltpu.VMEM(lead + (wire.full, 128), bf)
    little = lambda *lead: pltpu.VMEM(lead + (8, 128), f32)
    scratch = [
        big(nc), little(nc), big(nc), little(nc), big(plane - 1, line), little(plane - 1, line), big(line),
        little(line), big(line - 1), little(line - 1), little(), little(n - 1),
        dma((plane,)), dma((plane,)), dma, dma, dma((plane,)), dma((plane,)), dma((plane,)), dma((plane,)),
        dma((line,)), dma((line,)), dma((line,)), dma((line,)), dma((n,)), dma,
    ]
    return staged_call(
        functools.partial(reduce_kernel, wire), (grads, small), [((wire.full, 128), f32), ((n, 8, 128), f32)], scratch,
        functools.partial(greet_all, wire),
        vmem_limit_bytes=60 * 2**20, collective_id=1, has_side_effects=True, name="reduce_gradients")


def finish_kernel(
    wire, res, rows, qkv, proj, fc1, fc2, qkv_bias, proj_bias, fc1_bias, gain1, shift1, gain2, shift2, fc2_bias,
    pool_kernel, pool_gain, pool_bias, rel_h, rel_w,
):
    wide = wire.width
    a, b, c = wire.rows
    top, low = wire.unfold(res[...])
    qkv[...] = top[0:a]
    proj[...] = top[a:a + b]
    fc1[...] = top[a + b:wire.top]
    fc2[...] = jnp.concatenate([low[q * wire.low:(q + 1) * wire.low] for q in range(wire.parts)], 1)
    rel_h[...] = rows[0:REL, :HD]
    rel_w[...] = rows[64:64 + REL, :HD]
    for k in range(9):
        for w in range(2):
            pool_kernel[k, w:w + 1, :] = rows[128 + 9 * w + k:129 + 9 * w + k, :HD]
    pool_gain[...] = rows[146:148, :HD]
    pool_bias[...] = rows[148:150, :HD]
    at = 152
    qkv_bias[...] = jnp.concatenate([rows[at + g:at + g + 1, :HD] for g in range(6)], 1).reshape(3 * D)
    at = 158
    fc1_bias[...] = jnp.concatenate([rows[at + g:at + g + 1, :] for g in range(6)], 1).reshape(FF)
    at = 164
    for k, ref in enumerate((gain1, shift1, gain2, shift2, fc2_bias, proj_bias)):
        first = at + 2 * k
        ref[...] = jnp.concatenate([rows[first:first + 1, :], rows[first + 1:first + 2, :D - 128]], 1).reshape(D)


def finish(wire, res, rows):
    a, b, c = wire.rows
    wide = wire.width
    shapes = [(a, wide), (b, wide), (c, wide), (wire.low, wire.parts * wide), (3 * D,), (D,), (FF,)]
    shapes += [(D,)] * 5 + [(9, 2, HD), (2, HD), (2, HD), (REL, HD), (REL, HD)]
    return staged_call(
        functools.partial(finish_kernel, wire), (res, rows.reshape(-1, 128)), [(v, f32) for v in shapes], [],
        vmem_limit_bytes=60 * 2**20, name="split_gradients")


def compute(wire, block_input, key_crop, cotangent, consts):
    canvases = block_input.shape[0]
    whole = lambda v: pl.BlockSpec(v.shape, lambda i, n=v.ndim: (0,) * n)
    per = lambda: pl.BlockSpec((PAIR, D, NTOK), lambda i: (i, 0, 0))
    packed = [((wire.n, wire.full, 128), bf), ((wire.n * 8, 128), f32)]
    results = pl.pallas_call(
        functools.partial(kernel, wire, canvases // PAIR),
        grid=(canvases // PAIR,),
        in_specs=[pl.BlockSpec(memory_space=pltpu.SMEM), per(), per()] + [whole(v) for v in consts],
        out_specs=[per(), per()] + [pl.BlockSpec(s, lambda i, n=len(s): (0,) * n) for s, _ in packed],
        out_shape=[jax.ShapeDtypeStruct((canvases, D, NTOK), bf), jax.ShapeDtypeStruct((canvases, D, NTOK), f32)]
        + [jax.ShapeDtypeStruct(*s) for s in packed],
        scratch_shapes=[
            pltpu.VMEM((FEAT, FF), f32), pltpu.VMEM((D, 256), f32), pltpu.VMEM((FEAT, FF), f32),
            pltpu.VMEM((D, FF), f32), pltpu.VMEM((256, 256), f32), pltpu.VMEM((9, 4, 8, 128), f32),
            pltpu.VMEM((2, 4, 8, 128), f32), pltpu.VMEM((D, 128), f32), pltpu.VMEM((D, 16), f32),
            pltpu.VMEM((4 * D + FF, D), f32), pltpu.VMEM((wire.pad, D), f32),
            pltpu.VMEM((PAIR, 4, KVROWS, 128), f32),
            pltpu.VMEM((PAIR, 4, 272, 128), f32),
            pltpu.VMEM((PAIR, 4, NTOK, 128), f32),
            pltpu.VMEM((PAIR, 2, 256, 256), bf),
            pltpu.VMEM((PAIR, 2, 256, 256), bf),
            pltpu.VMEM((PAIR, 2, 256, 256), bf),
        ] + [
            pltpu.VMEM(v, bf) for rows, cols in ((FEAT, FF), (D, 256), (FEAT, FF), (D, FF))
            for v in ((canvases // PAIR, rows, PAIR * REST), (canvases * REST, cols))
        ],
        compiler_params=pltpu.CompilerParams(vmem_limit_bytes=60 * 2**20),
        name="block_step",
    )(key_crop, jnp.swapaxes(block_input, 1, 2), jnp.swapaxes(cotangent, 1, 2), *consts)
    out, ig, grads, small = results
    return jnp.swapaxes(out, 1, 2), jnp.swapaxes(ig, 1, 2), grads, small


def local(
    wire, block_input, token_crop, key_crop, first_gain, first_bias, qkv_weight, qkv_bias, pool_kernel, pool_gain,
    pool_bias, rel_height, rel_width, proj_weight, proj_bias, second_gain, second_bias, fc1_weight, fc1_bias,
    fc2_weight, fc2_bias, cotangent,
):
    consts = gather(
        wire, (qkv_weight, proj_weight, fc1_weight, fc2_weight),
        (qkv_bias, proj_bias, fc1_bias, first_gain, first_bias, second_gain, second_bias, fc2_bias,
         jnp.transpose(pool_kernel, (1, 0, 2)), pool_gain, pool_bias, rel_height, rel_width))
    out, ig, grads, small = compute(wire, block_input, key_crop, cotangent, consts)
    res, rows = reduce(wire, grads, small.reshape(wire.n, 8, 128))
    (qkv, proj, fc1, fc2, qkv_b, proj_b, fc1_b, gain1, shift1, gain2, shift2, fc2_b, taps, pool_g, pool_s, rel_h,
     rel_w) = finish(wire, res, rows)
    return (out, ig, gain1, shift1, qkv.T, qkv_b, jnp.transpose(taps, (1, 0, 2)), pool_g, pool_s, rel_h, rel_w,
            proj.T, proj_b, gain2, shift2, fc1.T, fc1_b, fc2.T, fc2_b)


def solution(mesh):
    rows = P(("dp", "fsdp"), None, None)
    ids = P(("dp", "fsdp"), None)
    block = P("fsdp", "dp")
    one = P()
    wire = Wire(mesh.shape["dp"], mesh.shape["fsdp"])
    return jax.shard_map(
        functools.partial(local, wire),
        mesh=mesh,
        in_specs=(rows, ids, ids, one, one, block, one, one, one, one, one, one, block, one, one, one, block, one,
                  block, one, rows),
        out_specs=(rows, rows, one, one, block, one, one, one, one, one, one, block, one, one, one, block, one,
                   block, one),
        check_vma=False,
    )
```

```python
import functools

import jax
import jax.numpy as jnp
from jax import lax
from jax.experimental import pallas as pl
from jax.experimental.pallas import tpu as pltpu
from jax.sharding import PartitionSpec as P

D = 192
HEADS = 2
HD = 96
FF = 768
SIDE = 28
KS = 14
NTOK = 784
NKEY = 196
REL = 55

EPS = 1e-06
FILL = -1e30
LOG2E = 1.4426950408889634
SCALE = HD ** (-0.5)
BASE = 32
KVROWS = BASE + NTOK + 24
bf = jnp.bfloat16
PAIR = 2
SKEW = 9
EVERY = 9
FEAT = 208
MAIN = 768
REST = 16
f32 = jnp.float32


def dot(a, b):
    return jnp.dot(a, b, preferred_element_type=f32)


def dot_nt(a, b):
    return lax.dot_general(a, b, (((1,), (1,)), ((), ())), preferred_element_type=f32)


def dot_tn(a, b):
    return lax.dot_general(a, b, (((0,), (0,)), ((), ())), preferred_element_type=f32)


def iota(shape, dim):
    return lax.broadcasted_iota(jnp.int32, shape, dim)


def widen(v):
    return jnp.concatenate([v, jnp.zeros((v.shape[0], 256 - v.shape[1]), v.dtype)], axis=1)


def lanes(col):
    return jnp.concatenate([col] * 6 + [col[:, :16]], axis=1)


def fold_lanes(v):
    total = v[:, 0:128]
    for n in range(1, 6):
        total = total + v[:, 128 * n:128 * n + 128]
    return total


def add_lanes(ref, tail, v):
    ref[...] += fold_lanes(v)
    tail[...] += v[:, 768:784]


def with_ones(v):
    extra = (iota((16, NTOK), 0) < 2).astype(f32).astype(bf)
    return jnp.concatenate([v, extra], 0)


def norm_cols(v):
    mean = jnp.sum(v, 0, keepdims=True) * (1.0 / D)
    c = v - mean
    var = jnp.sum(c * c, 0, keepdims=True) * (1.0 / D)
    r = lax.rsqrt(var + EPS)
    return c * r, r


def norm_cols_back(ge, u, r):
    s1 = jnp.sum(ge, 0, keepdims=True) * (1.0 / D)
    s2 = jnp.sum(ge * u, 0, keepdims=True) * (1.0 / D)
    return (ge - s1 - u * s2) * r


def fold(v):
    total = v[0:8]
    for n in range(1, v.shape[0] // 8):
        total = total + v[8 * n:8 * n + 8]
    return total


def norm_parts(v, mask, width):
    mean = jnp.sum(v, -1, keepdims=True) * (1.0 / width)
    c = (v - mean) * mask
    var = jnp.sum(c * c, -1, keepdims=True) * (1.0 / width)
    r = lax.rsqrt(var + EPS)
    return c * r, r


def norm_back(ge, u, r, width):
    s1 = jnp.sum(ge, -1, keepdims=True) * (1.0 / width)
    s2 = jnp.sum(ge * u, -1, keepdims=True) * (1.0 / width)
    return (ge - s1 - u * s2) * r


def roll_x(tile):
    out = []
    low = iota((8, 128), 0) < 4
    for p in range(KS):
        b = tile[56 * p:56 * p + 56]

        def by(v, n):
            return v if n == 0 else pltpu.roll(v, n, 1)

        out.append(by(b[0:24], 2 * p))
        out.append(jnp.where(low, by(b[24:32], 2 * p), by(b[24:32], 2 * p + 1)))
        out.append(by(b[32:56], 2 * p + 1))
    return out


def roll_y(tile):
    out = []
    low = iota((8, 128), 0) < 4
    for p in range(KS):
        b = tile[56 * p:56 * p + 56]
        out.append(pltpu.roll(b[0:24], 0, 1, stride=1, stride_axis=0))
        mid = b[24:32]
        first = pltpu.roll(mid, 24, 1, stride=1, stride_axis=0)
        second = pltpu.roll(pltpu.roll(mid, 124, 1), 0, 1, stride=1, stride_axis=0)
        out.append(jnp.where(low, first, second))
        out.append(pltpu.roll(b[32:56], 4, 1, stride=1, stride_axis=0))
    return out


def kernel(
    wire, steps_of, kc_ref, x_ref, g_ref, wq_ref, wpt_ref, w1_ref, w2t_ref, wqt_ref, wp_ref, w1t_ref, w2_ref,
    relf_ref, relb_ref, vec_ref, pk_ref, pv_ref,
    out_ref, ig_ref, wire_ref, small_ref,
    gq_ref, gp_ref, g1_ref, g2_ref, grel_ref, gpk_ref, gpv_ref, gln_ref, tail_ref, table, piece,
    kvs, gps, gkvs, kf, kb, vx, *spare,
):
    step = pl.program_id(0)
    spare = [(spare[2 * k], spare[2 * k + 1]) for k in range(4)]

    @pl.when(step == 0)
    def _():
        for ref in (gq_ref, gp_ref, g1_ref, g2_ref, grel_ref, gpk_ref, gpv_ref, gln_ref, tail_ref):
            ref[...] = jnp.zeros_like(ref)
        for c, n in [(c, n) for c in range(PAIR) for n in range(4)]:
            kvs[c, n, 0:BASE, :] = jnp.zeros((BASE, 128), f32)
            kvs[c, n, BASE + NTOK:KVROWS, :] = jnp.zeros((KVROWS - BASE - NTOK, 128), f32)
            gps[c, n, 224:272, :] = jnp.zeros((48, 128), f32)
        key = iota((256, 128), 0)
        lane = iota((256, 128), 1)
        ki = key >> 4
        kj = key & 15
        spot = lane & 63
        low = lane < 64
        real = (kj < KS) & (ki < KS)
        for c, h in [(c, h) for c in range(PAIR) for h in range(HEADS)]:
            first, second = (ki, kj) if h == 0 else (kj, ki)
            which = jnp.where(low, first, second)
            kf[c, h, :, 128:] = jnp.where((spot == 27 + 2 * which) & real, 1.0, 0.0).astype(bf)
            kb[c, h, :, 128:] = jnp.where((spot == 26 - 2 * which) & real, 1.0, 0.0).astype(bf)
            kf[c, h, :, :128] = jnp.where((lane == HD) & (key >= 0), FILL, 0.0).astype(bf)
            kb[c, h, :, :128] = jnp.zeros((256, 128), bf)
            vx[c, h, :, :128] = jnp.zeros((256, 128), bf)
            vx[c, h, :, 128:] = jnp.ones((256, 128), bf)

    pairs = Pairs(step, dict(gq=gq_ref, gp=gp_ref, g1=g1_ref, g2=g2_ref), dict(zip(("gq", "gp", "g1", "g2"), spare)))
    later = pairs.later
    steps = [
        canvas(
            pairs, step * PAIR + c, c, kc_ref, x_ref, g_ref, wq_ref, wpt_ref, w1_ref, w2t_ref, wqt_ref, wp_ref, w1t_ref, w2_ref,
            relf_ref, relb_ref, vec_ref, pk_ref, pv_ref,
            out_ref, ig_ref, gq_ref, gp_ref, g1_ref, g2_ref, grel_ref, gpk_ref, gpv_ref, gln_ref, tail_ref,
            kvs.at[c], gps.at[c], gkvs.at[c], kf.at[c], kb.at[c], vx.at[c])
        for c in range(PAIR)]
    live = list(steps)
    tick = 0
    while live:
        for c, one in enumerate(steps):
            if one in live and tick >= c * SKEW:
                try:
                    next(one)
                except StopIteration:
                    live.remove(one)
                if later and tick % EVERY == 0:
                    later.pop(0)()
        tick += 1
    while later:
        later.pop(0)()

    @pl.when(step == pl.num_programs(0) - 1)
    def _():
        pairs.finish(steps_of)
        pack(wire, wq_ref, w1_ref, vec_ref, wire_ref, small_ref, gq_ref, gp_ref, g1_ref, g2_ref, grel_ref, gpk_ref, gpv_ref, gln_ref,
             tail_ref, table, piece)


def pack(wire, wq_ref, w1_ref, vec_ref, wire_ref, small_ref, gq_ref, gp_ref, g1_ref, g2_ref, grel_ref, gpk_ref, gpv_ref, gln_ref, tail_ref,
         table, piece):
    wide = wire.width
    gain1, shift1, gain2, shift2 = [vec_ref[k] for k in range(4)]
    norm_rows = []
    for ref, w_ref, gain, shift in ((gq_ref, wq_ref, gain1, shift1), (g1_ref, w1_ref, gain2, shift2)):
        by_gain, by_shift = 0.0, 0.0
        for g in range(6):
            cols = slice(128 * g, 128 * g + 128)
            w = w_ref[:D, cols].astype(f32)
            sums = ref[D:D + 1, cols]
            by_gain = by_gain + w * ref[:D, cols]
            by_shift = by_shift + w * sums
            ref[:D, cols] = gain * ref[:D, cols] + shift * sums
        for v in (by_gain, by_shift):
            norm_rows.append(jnp.sum(jnp.transpose(v / gain), 0, keepdims=True))
    for g in range(6):
        table[HD * g:HD * g + HD, :] = jnp.transpose(gq_ref[:D, 128 * g:128 * g + 128])[:HD]
    table[3 * D:4 * D, :] = jnp.concatenate([gp_ref[:, 0:HD], gp_ref[:, 128:128 + HD]], 1)
    table[4 * D:4 * D + FF, :] = jnp.transpose(g1_ref[:D])
    piece[...] = jnp.zeros_like(piece)
    for d in range(wire.dp):
        for first, count, at in wire.starts(d):
            piece[first:first + count, :] = table[at:at + count, :]
        low = g2_ref[wire.low * d:wire.low * (d + 1), :] * 0.5
        for f in range(wire.fsdp):
            for q in range(wire.parts):
                first = wire.top + q * wire.low
                at = (f * wire.parts + q) * wide
                piece[first:first + wire.low, f * wide:(f + 1) * wide] = low[:, at:at + wide]
        for f in range(wire.fsdp):
            part = piece[:, f * wide:(f + 1) * wide]
            wire_ref[wire.slot(d, f)] = wire.fold(part[:wire.top], part[wire.top:wire.used]).astype(bf)
    small_ref[...] = jnp.zeros_like(small_ref)
    turned = jnp.transpose(grel_ref[...])
    small_ref[0:64] = turned[0:64, 0:128] + turned[64:128, 128:256]
    small_ref[64:128] = turned[192:256, 0:128] + turned[128:192, 128:256]
    for w in range(2):
        for k in range(9):
            small_ref[128 + 9 * w + k:129 + 9 * w + k] = jnp.sum(
                gpk_ref[k, 2 * w] + gpk_ref[k, 2 * w + 1], 0, keepdims=True)
        for m in range(2):
            small_ref[146 + 2 * m + w:147 + 2 * m + w] = jnp.sum(
                gpv_ref[m, 2 * w] + gpv_ref[m, 2 * w + 1], 0, keepdims=True)
    for g in range(6):
        small_ref[152 + g:153 + g] = gq_ref[D:D + 1, 128 * g:128 * g + 128]
        small_ref[158 + g:159 + g] = g1_ref[D:D + 1, 128 * g:128 * g + 128]
    rows = norm_rows + [jnp.sum(jnp.transpose(gln_ref[...]), 0, keepdims=True)
                        + jnp.sum(jnp.transpose(tail_ref[...]), 0, keepdims=True)]
    rows.append(jnp.transpose(gp_ref[:, 0:128])[HD:HD + 1])
    for k, v in enumerate(rows):
        small_ref[164 + 2 * k:165 + 2 * k] = v[:, 0:128]
        small_ref[165 + 2 * k:166 + 2 * k] = jnp.concatenate([v[:, 128:D], jnp.zeros((1, 256 - D), f32)], 1)


def features(v, w):
    return jnp.transpose(dot(v, w)[:, :D])


def add_dot(ref, cols, left, right):
    ref[:, cols] += dot(left, right)


class Pairs:
    def __init__(self, step, totals, spare):
        self.step, self.totals, self.spare = step, totals, spare
        self.later, self.held = [], {}

    def add(self, name, slot, left, right):
        self.held.setdefault(name, []).append((slot, left, right))
        if len(self.held[name]) < PAIR:
            return
        both = sorted(self.held.pop(name), key=lambda v: v[0])
        total = self.totals[name]
        left = jnp.concatenate([v[1][:, :MAIN] for v in both], 1)
        right = jnp.concatenate([v[2][:MAIN] for v in both], 0)
        for n in range(0, right.shape[1], 256):
            cols = slice(n, n + 256)
            self.later.append(functools.partial(add_dot, total, cols, left, right[:, cols]))
        keep_left, keep_right = self.spare[name]
        keep_left[self.step] = jnp.concatenate([v[1][:, MAIN:] for v in both], 1)
        rows = PAIR * REST
        keep_right[pl.ds(pl.multiple_of(self.step * rows, rows), rows), :] = jnp.concatenate([v[2][MAIN:] for v in both], 0)

    def finish(self, steps):
        for name, total in self.totals.items():
            keep_left, keep_right = self.spare[name]
            left = jnp.concatenate([keep_left[k] for k in range(steps)], 1)
            total[...] += dot(left, keep_right[...])


def canvas(
    pairs, item, slot, kc_ref, x_ref, g_ref, wq_ref, wpt_ref, w1_ref, w2t_ref, wqt_ref, wp_ref, w1t_ref, w2_ref,
    relf_ref, relb_ref, vec_ref, pk_ref, pv_ref,
    out_ref, ig_ref, gq_ref, gp_ref, g1_ref, g2_ref, grel_ref, gpk_ref, gpv_ref, gln_ref, tail_ref,
    kvs, gps, gkvs, kf, kb, vx,
):
    lane128 = iota((1, 128), 1)
    mask96 = (lane128 < HD).astype(f32)
    lowhalf = iota((NTOK, 128), 1) < 64

    fc2_bias = lanes(vec_ref[4])

    x = x_ref[slot].astype(f32)
    u1, r1 = norm_cols(x)
    nb = with_ones(u1.astype(bf))
    nt = jnp.transpose(nb)
    qb = dot(nt, wq_ref[:, :256]).astype(bf)
    for w in range(2):
        both = dot(nt, wq_ref[:, 256 + 256 * w:512 + 256 * w])
        kvs[2 * w, BASE:BASE + NTOK, :] = both[:, :128]
        kvs[2 * w + 1, BASE:BASE + NTOK, :] = both[:, 128:]

    yield
    notfirst = (iota((16, 128), 0) > 0).astype(f32)

    def tap(n, x_row, b):
        v = kvs.at[n][pl.ds(BASE + SIDE * x_row + b - 1, 16, stride=2), :]
        return v

    u_pool, r_pool = [], []
    for n in range(4):
        w = n // 2
        taps = [pk_ref[w, k:k + 1] for k in range(9)]
        taps = [v * notfirst if k % 3 == 0 else v for k, v in enumerate(taps)]
        rows = []
        for i in range(KS):
            acc = None
            for a in range(3):
                for b in range(3):
                    t = tap(n, 2 * i + a - 1, b) * taps[3 * a + b]
                    acc = t if acc is None else acc + t
            rows.append(acc)
        u, r = norm_parts(jnp.concatenate(rows, 0), mask96, HD)
        u_pool.append(u)
        r_pool.append(r)
        val = u * pv_ref[w:w + 1] + pv_ref[2 + w:3 + w]
        yield
        h = n % 2
        if w == 0:
            kb[h, 0:224, :128] = (val * SCALE).astype(bf)
            val = val * (SCALE * LOG2E)
            pad = ((iota((224, 128), 0) & 15) >= KS) & (iota((224, 128), 1) == HD)
            kf[h, 0:224, :128] = jnp.where(pad, FILL, val).astype(bf)
        else:
            vx[h, 0:224, :128] = val.astype(bf)

    row_cut = 0
    col_cut = 0
    for n in range(KS):
        row_cut = row_cut + jnp.where(kc_ref[item, KS * n] < 2, 2, 0)
        col_cut = col_cut + jnp.where((kc_ref[item, n] & 1) == 0, 2, 0)
    spot = (lane128 & 63) - 27
    row_side = spot >= row_cut
    col_side = spot >= col_cut
    rows_before = jnp.where(row_side, FILL, 0.0)
    rows_after = jnp.where(row_side, 0.0, FILL)
    y56 = iota((56, 128), 0)
    y56 = jnp.where(y56 >= SIDE, y56 - SIDE, y56)
    col_bias = jnp.where((y56 >= col_cut) != col_side, FILL, 0.0)

    yield
    a_both = dot(qb, relf_ref[...])
    a_h, a_w = a_both[:, :128], a_both[:, 128:]
    pieces_h = roll_x(a_h)
    yield
    pieces_w = roll_y(a_w)
    done_h, done_w = [], []
    for p in range(KS):
        row_bias = jnp.where(2 * p >= row_cut, rows_after, rows_before)
        done_h.append(jnp.concatenate(pieces_h[3 * p:3 * p + 3], 0) + row_bias)
        done_w.append(jnp.concatenate(pieces_w[3 * p:3 * p + 3], 0) + col_bias)
    yield
    t_h = jnp.concatenate(done_h, 0)
    t_w = jnp.concatenate(done_w, 0)
    rel = (jnp.where(lowhalf, t_h, t_w).astype(bf), jnp.where(lowhalf, t_w, t_h).astype(bf))

    yield
    eb, inv, mixed = [], [], []
    for h in range(HEADS):
        left = jnp.concatenate([qb[:, 128 * h:128 * h + 128], rel[h]], 1)
        s = dot_nt(left, kf[h])
        e = jnp.exp2(s - jnp.max(s, -1, keepdims=True)).astype(bf)
        yield
        o = dot(e, vx[h])
        rinv = 1.0 / o[:, 128:]
        eb.append(e)
        inv.append(rinv)
        mixed.append(o[:, :128] * rinv)
    yield
    ab = (jnp.concatenate(mixed, 1) + qb.astype(f32)).astype(bf)

    yield
    middle = x + dot_nt(wpt_ref[...], ab)
    u2, r2 = norm_cols(middle)
    n2b = with_ones(u2.astype(bf))
    gb = g_ref[slot]
    n2t, gt = jnp.transpose(n2b), jnp.transpose(gb)
    yield
    act, gh = [], []
    for n in range(3):
        cols = slice(256 * n, 256 * n + 256)
        hid = dot(n2t, w1_ref[:, cols])
        gact = dot(gt, w2t_ref[:, cols])
        yield
        hid = hid.astype(bf)
        z = hid * bf(0.7071067811865476)
        phi = bf(1.0) + lax.erf(z)
        slope = phi + z * (jnp.exp2(z * z * bf(-LOG2E)) * bf(1.1283791670955126))
        act.append(hid * phi)
        gh.append(gact.astype(bf) * slope)
        yield
    act = jnp.concatenate(act, 1)
    gh = jnp.concatenate(gh, 1)
    out = middle + fc2_bias + features(act, w2_ref[...])
    out_ref[slot] = out.astype(bf)
    pairs.add("g2", slot, gb, act)
    pairs.add("g1", slot, n2b, gh)
    yield
    g = gb.astype(f32)
    add_lanes(gln_ref, tail_ref, g)
    ge = features(gh, w1t_ref[...])
    yield
    gm = g + norm_cols_back(ge, u2, r2)
    grb = gm.astype(bf)
    pairs.add("gp", slot, grb, ab)
    yield
    yield
    gatt = dot_tn(grb, wpt_ref[...])
    gr, gcont = [], []
    g2bs, dss = [], []
    for h in range(HEADS):
        ga = gatt[:, 128 * h:128 * h + 128]
        ga = ga * inv[h]
        g2b = ga.astype(bf)
        dd = jnp.sum(ga * mixed[h], -1, keepdims=True)
        yield
        gpr = dot_nt(g2b, vx[h, :, :128])
        ds = eb[h] * (gpr - dd).astype(bf)
        yield
        back = dot(ds, kb[h])
        gcont.append(back[:, :128])
        gr.append(back[:, 128:])
        dss.append(ds)
        g2bs.append(g2b)
    yield
    b_h = jnp.concatenate(roll_x(jnp.where(lowhalf, gr[0], gr[1])), 0)
    yield
    b_w = jnp.concatenate(roll_y(jnp.where(lowhalf, gr[1], gr[0])), 0)
    gab = jnp.concatenate([b_h, b_w], 1).astype(bf)
    gq = jnp.concatenate(gcont, 1) + dot(gab, relb_ref[...]) + gatt

    yield
    for n in range(4):
        w, h = n // 2, n % 2
        if w == 0:
            qt = dot_tn(qb[:, 128 * h:128 * h + HD], jnp.concatenate([dss[h], gab], 1))
            grel_ref[128 * h:128 * h + HD] += qt[:, 256:]
            e = jnp.transpose(qt[:, :256])[:224] * SCALE
        else:
            e = jnp.transpose(dot_tn(g2bs[h][:, :HD], eb[h]))[:224]
        e = jnp.concatenate([e, jnp.zeros((224, 128 - HD), f32)], 1)
        yield
        gpv_ref[0, n] += fold(e * u_pool[n])
        gpv_ref[1, n] += fold(e)
        gps[n, 0:224, :] = norm_back(e * pv_ref[w:w + 1], u_pool[n], r_pool[n], HD)

    for n in range(4):
        w = n // 2
        for a in range(3):
            yield
            for b in range(3):
                acc = None
                for i in range(KS):
                    t = gps[n, 16 * i:16 * i + 16, :] * tap(n, 2 * i + a - 1, b)
                    acc = t if acc is None else acc + t
                if b == 0:
                    acc = acc * notfirst
                gpk_ref[3 * a + b, n] += acc[0:8] + acc[8:16]


        yield
        def wk(a, b):
            return pk_ref[w, 3 * a + b:3 * a + b + 1]

        for i in range(KS):
            p0 = gps[n, 16 * i:16 * i + 16, :]
            p0s = gps[n, 16 * i + 1:16 * i + 17, :]
            p1 = gps[n, 16 * i + 16:16 * i + 32, :]
            p1s = gps[n, 16 * i + 17:16 * i + 33, :]
            even = SIDE * 2 * i
            odd = even + SIDE
            ee = p0 * wk(1, 1)
            eo = p0 * wk(1, 2) + p0s * wk(1, 0)
            oe = p0 * wk(2, 1) + p1 * wk(0, 1)
            oo = p0 * wk(2, 2) + p0s * wk(2, 0) + p1 * wk(0, 2) + p1s * wk(0, 0)
            gk = gkvs.at[n]
            gk[pl.ds(even, KS, stride=2), :] = ee[:KS]
            gk[pl.ds(even + 1, KS, stride=2), :] = eo[:KS]
            gk[pl.ds(odd, KS, stride=2), :] = oe[:KS]
            gk[pl.ds(odd + 1, KS, stride=2), :] = oo[:KS]

    yield
    gpk = jnp.concatenate([gq.astype(bf)] + [gkvs[n].astype(bf) for n in range(4)], 1)
    pairs.add("gq", slot, nb, gpk)
    ge = features(gpk, wqt_ref[...])
    yield
    ig_ref[slot] = gm + norm_cols_back(ge, u1, r1)


MESH = pl.DeviceIdType.MESH


class Wire:
    def __init__(self, dp, fsdp):
        self.dp, self.fsdp, self.n = dp, fsdp, dp * fsdp
        self.chips = self.n // 2
        self.line, self.plane = dp // 4, 2 * fsdp
        self.rows = (3 * D // dp, D // dp, FF // dp)
        self.top = sum(self.rows)
        self.low = D // dp
        self.width = D // fsdp
        self.parts = FF // fsdp // self.width
        self.used = self.top + self.parts * self.low
        self.pad = -(-self.used // 16) * 16
        self.tile = 128 if FF // fsdp % 128 == 0 else FF // fsdp
        self.tiles = FF // fsdp // self.tile
        self.load = -(-(self.top + self.tiles * self.low) // 16) * 16
        self.lows = self.parts * self.low
        self.dense = self.width == 96 and self.top == 2 * self.lows and self.lows % 48 == 0
        self.full = self.top + self.lows // 3 if self.dense else self.pad

    def fold(self, top, low, *more):
        rows = self.lows
        if self.dense:
            third = rows // 3
            parts = [
                jnp.concatenate([top[:rows], low[:, 0:32]], 1),
                jnp.concatenate([top[rows:], low[:, 32:64]], 1),
                jnp.concatenate([low[k * third:(k + 1) * third, 64:96] for k in range(3)]
                                + [jnp.zeros((third, 32), top.dtype)], 1)]
        else:
            parts = [jnp.concatenate([v, jnp.zeros((v.shape[0], 128 - self.width), top.dtype)], 1) for v in (top, low)]
            if self.pad > self.used:
                parts.append(jnp.zeros((self.pad - self.used, 128), top.dtype))
        return jnp.concatenate(parts + list(more), 0)

    def unfold(self, block):
        rows, wide = self.lows, self.width
        if not self.dense:
            return block[:self.top, :wide], block[self.top:self.used, :wide]
        third = rows // 3
        last = jnp.concatenate([block[self.top:self.top + third, 32 * k:32 * k + 32] for k in range(3)], 0)
        low = jnp.concatenate([block[:rows, 96:128], block[rows:2 * rows, 96:128], last], 1)
        return block[:self.top, :wide], low

    def starts(self, d):
        a, b, c = self.rows
        return ((0, a, a * d), (a, b, 3 * D + b * d), (a + b, c, 4 * D + c * d))

    def slot(self, d, f):
        return (d % 2) * self.chips + ((d // 2) % 2 * self.fsdp + f) * self.line + d // 4

    def place(self):
        d, f = lax.axis_index("dp"), lax.axis_index("fsdp")
        return lax.rem(d, 2), lax.rem(d // 2, 2) * self.fsdp + f, d // 4

    def peer(self, slot):
        chip = lax.rem(slot, self.chips)
        return self.device(slot // self.chips, chip // self.line, lax.rem(chip, self.line))

    def device(self, core, q, z):
        return (4 * z + 2 * (q // self.fsdp) + core, lax.rem(q, self.fsdp))


def greet_near(wire):
    line, plane = wire.line, wire.plane
    core, q, z = wire.place()
    friends = [wire.device(1 - core, q, z)]
    friends += [wire.device(core, q, lax.rem(z + k, line)) for k in range(1, line)]
    friends += [wire.device(core, lax.rem(q + j, plane), z) for j in range(1, plane)]
    for friend in friends:
        pl.semaphore_signal(pltpu.get_barrier_semaphore(), inc=1, device_id=friend, device_id_type=MESH)


def gather_kernel(
    wire, qkv, proj, fc1, fc2, qkv_bias, proj_bias, fc1_bias, gain1, shift1, gain2, shift2, fc2_bias,
    pool_kernel, pool_gain, pool_bias, rel_h, rel_w,
    wq_ref, wpt_ref, w1_ref, w2t_ref, wqt_ref, wp_ref, w1t_ref, w2_ref, relf_ref, relb_ref, vec_ref, pk_ref, pv_ref,
    buf, tmp, table, low_table, line_send, plane_send, core_send, recv,
):
    nc, line, plane = wire.chips, wire.line, wire.plane
    core, q, z = wire.place()
    other = 1 - core
    me = core * nc + q * line + z
    wide = wire.width
    a, b, c = wire.rows
    tmp[...] = jnp.zeros_like(tmp)
    tmp[0:a, :wide] = qkv[...].astype(f32)
    tmp[a:a + b, :wide] = proj[...].astype(f32)
    tmp[a + b:wire.top, :wide] = fc1[...].astype(f32)
    below = fc2[...].astype(f32)
    for p in range(wire.tiles):
        first = wire.top + p * wire.low
        tmp[first:first + wire.low, :wire.tile] = below[:, p * wire.tile:(p + 1) * wire.tile]
    buf[pl.ds(me, 1)] = tmp[...].astype(bf)[None]
    pl.semaphore_wait(pltpu.get_barrier_semaphore(), line + plane - 1)

    def held(k, j):
        return core * nc + lax.rem(q + j, plane) * line + lax.rem(z + k, line)

    def copy(slot, sem, device):
        return pltpu.make_async_remote_copy(
            src_ref=buf.at[slot], dst_ref=buf.at[slot], send_sem=sem, recv_sem=recv.at[slot],
            device_id=device, device_id_type=MESH)

    def to_line(k):
        return copy(me, line_send.at[k], wire.device(core, q, lax.rem(z + k, line)))

    def to_plane(k, j):
        return copy(held(k, 0), plane_send.at[k * plane + j], wire.device(core, lax.rem(q + j, plane), z))

    def to_core(k, j):
        return copy(held(k, j), core_send.at[k * plane + j], wire.device(other, q, z))

    for k in range(1, line):
        to_line(k).start()
    for j in range(1, plane):
        to_plane(0, j).start()
    to_core(0, 0).start()

    def row(ref):
        return ref[...].reshape(1, ref.shape[0])

    for k, ref in enumerate((gain1, shift1, gain2, shift2, fc2_bias)):
        vec_ref[k] = jnp.transpose(jnp.broadcast_to(row(ref), (128, D)))
    zero32 = jnp.zeros((64, 128 - HD), f32)

    def tall(ref):
        t = jnp.concatenate([ref[...], jnp.zeros((64 - REL, HD), f32)], 0)
        t = jnp.concatenate([t, zero32], 1)
        return jnp.where(iota((64, 128), 0) < 54, t, 0.0)

    th, tw = tall(rel_h), tall(rel_w)
    none = jnp.zeros((64, 128), f32)
    relb = jnp.concatenate([
        jnp.concatenate([th, none], 1), jnp.concatenate([none, th], 1),
        jnp.concatenate([none, tw], 1), jnp.concatenate([tw, none], 1)], 0)
    relb_ref[...] = relb.astype(bf)
    at, to = iota((256, 256), 0), iota((256, 256), 1)
    mirror = ((at >> 6) == (to >> 6)) & ((at & 63) + (to & 63) == 53)
    relf_ref[...] = dot_tn((relb * LOG2E).astype(bf), jnp.where(mirror, 1.0, 0.0).astype(bf)).astype(bf)
    for w in range(2):
        taps = jnp.concatenate([pool_kernel[k, w:w + 1, :] for k in range(9)], 0)
        pk_ref[w] = jnp.concatenate([taps, jnp.zeros((9, 128 - HD), f32)], 1)
    four = jnp.concatenate([pool_gain[...], pool_bias[...]], 0)
    pv_ref[...] = jnp.concatenate([four, jnp.zeros((4, 128 - HD), f32)], 1)

    for k in range(1, line):
        to_core(k, 0).wait_recv()
        for j in range(1, plane):
            to_plane(k, j).start()
        to_core(k, 0).start()
    for k in range(line):
        for j in range(1, plane):
            to_core(k, j).wait_recv()
            to_core(k, j).start()
    for c in range(nc):
        copy(other * nc + c, core_send.at[0], wire.device(other, q, z)).wait_recv()

    for d in range(wire.dp):
        blocks = [buf[wire.slot(d, f)].astype(f32) for f in range(wire.fsdp)]
        top = jnp.concatenate([v[:wire.top, :wide] for v in blocks], 1)
        for first, count, to_row in wire.starts(d):
            table[to_row:to_row + count, :] = top[first:first + count, :]
        for f, v in enumerate(blocks):
            for p in range(wire.tiles):
                first, at = wire.top + p * wire.low, (f * wire.tiles + p) * wire.tile
                low_table[wire.low * d:wire.low * (d + 1), at:at + wire.tile] = v[first:first + wire.low, :wire.tile]

    def two(bias):
        hi = bias.astype(bf).astype(f32)
        return jnp.concatenate([hi, bias - hi, jnp.zeros((14, bias.shape[1]), f32)], 0)

    qb = row(qkv_bias)
    for g in range(6):
        w = jnp.transpose(table[HD * g:HD * g + HD, :])
        bias = qb[:, HD * g:HD * g + HD] + jnp.sum(w * vec_ref[1][:, :HD], 0, keepdims=True)
        block = jnp.concatenate([w * vec_ref[0][:, :HD], two(bias)], 0)
        spare = (iota((FEAT, 128 - HD), 0) == D) & (iota((FEAT, 128 - HD), 1) == 0) & (g < 2)
        block = jnp.concatenate([block, jnp.where(spare, 1.0, 0.0)], 1)
        wq_ref[:, 128 * g:128 * g + 128] = block.astype(bf)
        flat = table[HD * g:HD * g + HD, :] * row(gain1)
        flat = jnp.concatenate([flat, jnp.zeros((128 - HD, D), f32)], 0)
        wqt_ref[128 * g:128 * g + 128, :] = widen(flat).astype(bf)
    cols = []
    pb = row(proj_bias)
    hi = pb.astype(bf).astype(f32)
    for g, extra in enumerate((hi, pb - hi)):
        col = jnp.transpose(jnp.broadcast_to(extra, (128, D)))[:, :128 - HD]
        col = jnp.where(iota((D, 128 - HD), 1) == 0, col, 0.0)
        cols += [table[3 * D:4 * D, HD * g:HD * g + HD], col]
    wpt = jnp.concatenate(cols, 1)
    wpt_ref[...] = wpt.astype(bf)
    wp_ref[...] = widen(jnp.transpose(wpt)).astype(bf)
    w1t_ref[...] = widen(table[4 * D:4 * D + FF, :] * row(gain2)).astype(bf)
    w2_ref[...] = widen(jnp.transpose(low_table[...]) * 0.5).astype(bf)
    fb = row(fc1_bias)
    for g in range(6):
        w = jnp.transpose(table[4 * D + 128 * g:4 * D + 128 * g + 128, :])
        bias = fb[:, 128 * g:128 * g + 128] + jnp.sum(w * vec_ref[3], 0, keepdims=True)
        w1_ref[:, 128 * g:128 * g + 128] = jnp.concatenate([w * vec_ref[2], two(bias)], 0).astype(bf)
    w2t_ref[...] = (low_table[...] * 0.5).astype(bf)

    for k in range(line):
        if k:
            to_line(k).wait_send()
        for j in range(plane):
            if j:
                to_plane(k, j).wait_send()
            to_core(k, j).wait_send()


def staged(body, hello, ins, outs, *refs):
    a, b = len(ins), len(outs)
    src, dst = refs[:a], refs[a:a + b]
    vin, vout = refs[a + b:2 * a + b], refs[2 * a + b:2 * (a + b)]
    sems, rest = refs[2 * (a + b)], refs[2 * (a + b) + 1:]
    hello()
    loads = [pltpu.make_async_copy(s, v, sems.at[k]) for k, (s, v) in enumerate(zip(src, vin))]
    for c in loads:
        c.start()
    for c in loads:
        c.wait()
    body(*vin, *vout, *rest)
    stores = [pltpu.make_async_copy(v, d, sems.at[k]) for k, (v, d) in enumerate(zip(vout, dst))]
    for c in stores:
        c.start()
    for c in stores:
        c.wait()


def staged_call(body, args, shapes, scratch, hello=lambda: None, **params):
    hbm = pl.BlockSpec(memory_space=pltpu.HBM)
    ins = [(v.shape, v.dtype) for v in args]
    name = params.pop("name")
    return pl.pallas_call(
        functools.partial(staged, body, hello, ins, shapes),
        in_specs=[hbm] * len(ins),
        out_specs=[hbm] * len(shapes),
        out_shape=[jax.ShapeDtypeStruct(*s) for s in shapes],
        scratch_shapes=[pltpu.VMEM(*s) for s in ins + list(shapes)]
        + [pltpu.SemaphoreType.DMA((max(len(ins), len(shapes)),))] + list(scratch),
        compiler_params=pltpu.CompilerParams(**params),
        name=name,
    )(*args)


def gather(wire, shards, vectors):
    shapes = [((FEAT, FF), bf), ((D, 256), bf), ((FEAT, FF), bf), ((D, FF), bf), ((FF, 256), bf), ((256, 256), bf), ((FF, 256), bf), ((FF, 256), bf),
              ((256, 256), bf), ((256, 256), bf),
              ((5, D, 128), f32), ((2, 9, 128), f32), ((4, 128), f32)]
    args = [v.T for v in shards] + list(vectors)
    scratch = [
        pltpu.VMEM((wire.n, wire.load, 128), bf),
        pltpu.VMEM((wire.load, 128), f32),
        pltpu.VMEM((4 * D + FF, D), f32),
        pltpu.VMEM((D, FF), f32),
        pltpu.SemaphoreType.DMA((wire.line,)),
        pltpu.SemaphoreType.DMA((wire.chips,)),
        pltpu.SemaphoreType.DMA((wire.chips,)),
        pltpu.SemaphoreType.DMA((wire.n,)),
    ]
    return staged_call(
        functools.partial(gather_kernel, wire), args, shapes, scratch, functools.partial(greet_near, wire),
        vmem_limit_bytes=60 * 2**20, collective_id=0, has_side_effects=True, name="gather_weights")


def greet_all(wire):
    core, q, z = wire.place()
    me = core * wire.chips + q * wire.line + z

    def one(k, c):
        pl.semaphore_signal(pltpu.get_barrier_semaphore(), inc=1, device_id=wire.peer(lax.rem(me + k, wire.n)),
                            device_id_type=MESH)
        return c

    lax.fori_loop(1, wire.n, one, 0)


def reduce_kernel(
    wire, grads, small, res_ref, sum_ref,
    abuf, sa, comb, scomb, bbuf, sb, comb2, scomb2, cbuf, sc, own, gsm,
    asend, arecv, sasend, sarecv, bsend, brecv, sbsend, sbrecv, csend, crecv, scsend, screcv, gsend, grecv,
):
    n, nc, line, plane = wire.n, wire.chips, wire.line, wire.plane
    core, q, z = wire.place()
    other = 1 - core
    me = core * nc + q * line + z

    def peer(k):
        return wire.peer(lax.rem(me + k, n))

    def loop(lo, hi, fn):
        def body(k, c):
            fn(k)
            return c
        lax.fori_loop(lo, hi, body, 0)

    pl.semaphore_wait(pltpu.get_barrier_semaphore(), n - 1)

    def remote(src, dst, send, recv, device):
        return pltpu.make_async_remote_copy(
            src_ref=src, dst_ref=dst, send_sem=send, recv_sem=recv, device_id=device, device_id_type=MESH)

    def plane_at(j):
        return lax.rem(q + j, plane)

    def line_at(k):
        return lax.rem(z + k, line)

    partner = wire.device(other, q, z)
    small_a = remote(small.at[pl.ds(other * nc, nc)], sa, sasend, sarecv, partner)

    def half(j):
        at = plane_at(j) * line
        return remote(grads.at[pl.ds(other * nc + at, line)], abuf.at[pl.ds(at, line)], asend.at[j], arecv.at[j], partner)

    def group(j):
        return remote(comb.at[pl.ds(plane_at(j) * line, line)], bbuf.at[j - 1], bsend.at[j], brecv.at[j],
                      wire.device(core, plane_at(j), z))

    def small_b(j):
        return remote(scomb.at[pl.ds(plane_at(j) * line, line)], sb.at[j - 1], sbsend.at[j], sbrecv.at[j],
                      wire.device(core, plane_at(j), z))

    def last(k):
        return remote(comb2.at[line_at(k)], cbuf.at[k - 1], csend.at[k], crecv.at[k], wire.device(core, q, line_at(k)))

    def small_c(k):
        return remote(scomb2.at[line_at(k)], sc.at[k - 1], scsend.at[k], screcv.at[k],
                      wire.device(core, q, line_at(k)))

    def spread(k):
        return remote(own, gsm.at[n - 1 - k], gsend.at[k], grecv, peer(k))

    order = list(range(1, plane)) + [0]
    small_a.start()
    for j in order:
        half(j).start()
    small_a.wait_recv()
    scomb[...] = small[pl.ds(core * nc, nc)] + sa[...]
    for j in range(1, plane):
        small_b(j).start()
    for j in order:
        half(j).wait_recv()
        at = pl.ds(plane_at(j) * line, line)
        both = grads[pl.ds(core * nc + plane_at(j) * line, line)].astype(f32) + abuf[at].astype(f32)
        comb[at] = both.astype(bf)
        if j:
            group(j).start()
    mine = pl.ds(q * line, line)
    total = scomb[mine]
    for j in range(1, plane):
        small_b(j).wait_recv()
        total = total + sb[j - 1]
    scomb2[...] = total
    for k in range(1, line):
        small_c(k).start()
    total = scomb2[pl.ds(z, 1)][0]
    for k in range(1, line):
        small_c(k).wait_recv()
        total = total + sc[k - 1]
    own[...] = total
    loop(1, n, lambda k: spread(k).start())
    total = comb[mine].astype(f32)
    for j in range(1, plane):
        group(j).wait_recv()
        total = total + bbuf[j - 1].astype(f32)
    comb2[...] = total.astype(bf)
    for k in range(1, line):
        last(k).start()
    total = comb2[pl.ds(z, 1)][0].astype(f32)
    for k in range(1, line):
        last(k).wait_recv()
        total = total + cbuf[k - 1].astype(f32)
    res_ref[...] = total
    pltpu.make_async_copy(gsm, gsm, grecv).wait()
    sum_ref[pl.ds(me, 1)] = own[...][None]

    def keep(k):
        sum_ref[pl.ds(lax.rem(me + n - k, n), 1)] = gsm[pl.ds(n - 1 - k, 1)]

    loop(1, n, keep)
    small_a.wait_send()
    for j in range(plane):
        half(j).wait_send()
        if j:
            group(j).wait_send()
            small_b(j).wait_send()
    for k in range(1, line):
        last(k).wait_send()
        small_c(k).wait_send()
    loop(1, n, lambda k: spread(k).wait_send())


def reduce(wire, grads, small):
    n, nc, line, plane = wire.n, wire.chips, wire.line, wire.plane
    dma = pltpu.SemaphoreType.DMA
    big = lambda *lead: pltpu.VMEM(lead + (wire.full, 128), bf)
    little = lambda *lead: pltpu.VMEM(lead + (8, 128), f32)
    scratch = [
        big(nc), little(nc), big(nc), little(nc), big(plane - 1, line), little(plane - 1, line), big(line),
        little(line), big(line - 1), little(line - 1), little(), little(n - 1),
        dma((plane,)), dma((plane,)), dma, dma, dma((plane,)), dma((plane,)), dma((plane,)), dma((plane,)),
        dma((line,)), dma((line,)), dma((line,)), dma((line,)), dma((n,)), dma,
    ]
    return staged_call(
        functools.partial(reduce_kernel, wire), (grads, small), [((wire.full, 128), f32), ((n, 8, 128), f32)], scratch,
        functools.partial(greet_all, wire),
        vmem_limit_bytes=60 * 2**20, collective_id=1, has_side_effects=True, name="reduce_gradients")


def finish_kernel(
    wire, res, rows, qkv, proj, fc1, fc2, qkv_bias, proj_bias, fc1_bias, gain1, shift1, gain2, shift2, fc2_bias,
    pool_kernel, pool_gain, pool_bias, rel_h, rel_w,
):
    wide = wire.width
    a, b, c = wire.rows
    top, low = wire.unfold(res[...])
    qkv[...] = top[0:a]
    proj[...] = top[a:a + b]
    fc1[...] = top[a + b:wire.top]
    fc2[...] = jnp.concatenate([low[q * wire.low:(q + 1) * wire.low] for q in range(wire.parts)], 1)
    rel_h[...] = rows[0:REL, :HD]
    rel_w[...] = rows[64:64 + REL, :HD]
    for k in range(9):
        for w in range(2):
            pool_kernel[k, w:w + 1, :] = rows[128 + 9 * w + k:129 + 9 * w + k, :HD]
    pool_gain[...] = rows[146:148, :HD]
    pool_bias[...] = rows[148:150, :HD]
    at = 152
    qkv_bias[...] = jnp.concatenate([rows[at + g:at + g + 1, :HD] for g in range(6)], 1).reshape(3 * D)
    at = 158
    fc1_bias[...] = jnp.concatenate([rows[at + g:at + g + 1, :] for g in range(6)], 1).reshape(FF)
    at = 164
    for k, ref in enumerate((gain1, shift1, gain2, shift2, fc2_bias, proj_bias)):
        first = at + 2 * k
        ref[...] = jnp.concatenate([rows[first:first + 1, :], rows[first + 1:first + 2, :D - 128]], 1).reshape(D)


def finish(wire, res, rows):
    a, b, c = wire.rows
    wide = wire.width
    shapes = [(a, wide), (b, wide), (c, wide), (wire.low, wire.parts * wide), (3 * D,), (D,), (FF,)]
    shapes += [(D,)] * 5 + [(9, 2, HD), (2, HD), (2, HD), (REL, HD), (REL, HD)]
    return staged_call(
        functools.partial(finish_kernel, wire), (res, rows.reshape(-1, 128)), [(v, f32) for v in shapes], [],
        vmem_limit_bytes=60 * 2**20, name="split_gradients")


def compute(wire, block_input, key_crop, cotangent, consts):
    canvases = block_input.shape[0]
    whole = lambda v: pl.BlockSpec(v.shape, lambda i, n=v.ndim: (0,) * n)
    per = lambda: pl.BlockSpec((PAIR, D, NTOK), lambda i: (i, 0, 0))
    packed = [((wire.n, wire.full, 128), bf), ((wire.n * 8, 128), f32)]
    results = pl.pallas_call(
        functools.partial(kernel, wire, canvases // PAIR),
        grid=(canvases // PAIR,),
        in_specs=[pl.BlockSpec(memory_space=pltpu.SMEM), per(), per()] + [whole(v) for v in consts],
        out_specs=[per(), per()] + [pl.BlockSpec(s, lambda i, n=len(s): (0,) * n) for s, _ in packed],
        out_shape=[jax.ShapeDtypeStruct((canvases, D, NTOK), bf), jax.ShapeDtypeStruct((canvases, D, NTOK), f32)]
        + [jax.ShapeDtypeStruct(*s) for s in packed],
        scratch_shapes=[
            pltpu.VMEM((FEAT, FF), f32), pltpu.VMEM((D, 256), f32), pltpu.VMEM((FEAT, FF), f32),
            pltpu.VMEM((D, FF), f32), pltpu.VMEM((256, 256), f32), pltpu.VMEM((9, 4, 8, 128), f32),
            pltpu.VMEM((2, 4, 8, 128), f32), pltpu.VMEM((D, 128), f32), pltpu.VMEM((D, 16), f32),
            pltpu.VMEM((4 * D + FF, D), f32), pltpu.VMEM((wire.pad, D), f32),
            pltpu.VMEM((PAIR, 4, KVROWS, 128), f32),
            pltpu.VMEM((PAIR, 4, 272, 128), f32),
            pltpu.VMEM((PAIR, 4, NTOK, 128), f32),
            pltpu.VMEM((PAIR, 2, 256, 256), bf),
            pltpu.VMEM((PAIR, 2, 256, 256), bf),
            pltpu.VMEM((PAIR, 2, 256, 256), bf),
        ] + [
            pltpu.VMEM(v, bf) for rows, cols in ((FEAT, FF), (D, 256), (FEAT, FF), (D, FF))
            for v in ((canvases // PAIR, rows, PAIR * REST), (canvases * REST, cols))
        ],
        compiler_params=pltpu.CompilerParams(vmem_limit_bytes=60 * 2**20),
        name="block_step",
    )(key_crop, jnp.swapaxes(block_input, 1, 2), jnp.swapaxes(cotangent, 1, 2), *consts)
    out, ig, grads, small = results
    return jnp.swapaxes(out, 1, 2), jnp.swapaxes(ig, 1, 2), grads, small


def local(
    wire, block_input, token_crop, key_crop, first_gain, first_bias, qkv_weight, qkv_bias, pool_kernel, pool_gain,
    pool_bias, rel_height, rel_width, proj_weight, proj_bias, second_gain, second_bias, fc1_weight, fc1_bias,
    fc2_weight, fc2_bias, cotangent,
):
    consts = gather(
        wire, (qkv_weight, proj_weight, fc1_weight, fc2_weight),
        (qkv_bias, proj_bias, fc1_bias, first_gain, first_bias, second_gain, second_bias, fc2_bias,
         jnp.transpose(pool_kernel, (1, 0, 2)), pool_gain, pool_bias, rel_height, rel_width))
    out, ig, grads, small = compute(wire, block_input, key_crop, cotangent, consts)
    res, rows = reduce(wire, grads, small.reshape(wire.n, 8, 128))
    (qkv, proj, fc1, fc2, qkv_b, proj_b, fc1_b, gain1, shift1, gain2, shift2, fc2_b, taps, pool_g, pool_s, rel_h,
     rel_w) = finish(wire, res, rows)
    return (out, ig, gain1, shift1, qkv.T, qkv_b, jnp.transpose(taps, (1, 0, 2)), pool_g, pool_s, rel_h, rel_w,
            proj.T, proj_b, gain2, shift2, fc1.T, fc1_b, fc2.T, fc2_b)


def solution(mesh):
    rows = P(("dp", "fsdp"), None, None)
    ids = P(("dp", "fsdp"), None)
    block = P("fsdp", "dp")
    one = P()
    wire = Wire(mesh.shape["dp"], mesh.shape["fsdp"])
    return jax.shard_map(
        functools.partial(local, wire),
        mesh=mesh,
        in_specs=(rows, ids, ids, one, one, block, one, one, one, one, one, one, block, one, one, one, block, one,
                  block, one, rows),
        out_specs=(rows, rows, one, one, block, one, one, one, one, one, one, block, one, one, one, block, one,
                   block, one),
        check_vma=False,
    )
```
